32 devices in a mesh: grp: 4 (over x, core), dev: 8 (over z, y).
Axes of the slice: x: 2, y: 2, z: 4, core: 2. Of those that a mesh axis runs over, the one named last changes fastest.
Arguments:
- solid_mask: int32 [96, 256, 128], P('grp', 'dev'), may hold values 0 or 1
- forcing: float32 [3, 96, 256, 128], P(None, 'grp', 'dev'), may hold values from -18 to 18
Outputs:
- velocity: float32 [3, 96, 256, 128], P(None, 'grp', 'dev')
- pressure: float32 [96, 256, 128], P('grp', 'dev')
The draws below stay inside these ranges and needn't reach their ends.
All inputs are finite; a program needn't handle non-finite values. No bound on the sum of `solid_mask` on one device may be relied on, other than what follows from the above.
Results may differ from the reference program's by a relative error of at most 0.000073.
Values sent between devices are 32-bit elements; how exact they have to be, the bound alone decides.
No kernel may reach another device: no remote copies, remote signals or barrier semaphores. Data moves between devices by JAX's collectives and lax.ppermute only.
A program may use at most 192 MiB of HBM per device.

```python
import jax
import jax.numpy as jnp
from jax import lax

NX = 96
NY = 256
NZ = 128


def place_ends(values, key, low, largest):
    extent = values.shape
    spot = [jax.random.randint(jax.random.fold_in(key, axis), (), 0, extent[axis]) for axis in range(len(extent))]
    values = values.at[tuple(spot)].set(low)
    longest = extent.index(max(extent))
    spot[longest] = (spot[longest] + 1) % extent[longest]
    return values.at[tuple(spot)].set(largest)


def block_scale(key, extent, cuts, least, top_value):
    def one(position, shards_of):
        steps = jax.random.uniform(jax.random.fold_in(jax.random.fold_in(key, 6), position), (shards_of,), jnp.float32, least / len(cuts), top_value / len(cuts))
        return jnp.repeat(jnp.exp(steps), extent[position] // shards_of).reshape((-1,) + (1,) * (len(extent) - position - 1))

    loudness = one(*cuts[0])
    for cut in cuts[1:]:
        loudness = loudness * one(*cut)
    return loudness


def gaussian(stream_key, extent, scale, bound, split=(), held_as=jnp.bfloat16):
    entries = scale * jax.random.normal(stream_key, extent, jnp.float32)
    if split:
        entries = entries * block_scale(stream_key, extent, split, -0.22, 0.18)
    return jnp.clip(entries, -bound, bound).astype(held_as)


def setup_inputs(seed: int = 0) -> dict:
    keys = jax.random.split(jax.random.key(seed), 3)
    solid_mask = place_ends((jax.random.randint(keys[0], (NX, NY, NZ), 0, 3) < 1).astype(jnp.int32), jax.random.fold_in(keys[0], 1), 0, 1)
    forcing = gaussian(keys[1], (3, NX, NY, NZ), 3.0, 18.0, ((1, 4), (2, 8)), jnp.float32)
    return dict(solid_mask=solid_mask, forcing=forcing)


viscosity = 1.0
penalty = 10.0
relaxation = 0.8
pressure_step = 1.0
mean_drive = 1.0


def trim_plane(field, width):
    return field[..., width:field.shape[-3] - width, width:field.shape[-2] - width, :]


def laplace(field, spacing):
    middle = trim_plane(field, 1)
    summed = field[..., 2:, 1:-1, :] + field[..., :-2, 1:-1, :] + field[..., 1:-1, 2:, :] + field[..., 1:-1, :-2, :]
    summed = summed + jnp.roll(middle, 1, -1) + jnp.roll(middle, -1, -1) - 6.0 * middle
    return summed / (spacing * spacing)


def gradient(field, spacing):
    middle = trim_plane(field, 1)
    along_x = field[2:, 1:-1, :] - field[:-2, 1:-1, :]
    along_y = field[1:-1, 2:, :] - field[1:-1, :-2, :]
    along_z = jnp.roll(middle, -1, -1) - jnp.roll(middle, 1, -1)
    return jnp.stack([along_x, along_y, along_z]) / (2.0 * spacing)


def divergence(field, spacing):
    middle = field[2, 1:-1, 1:-1, :]
    summed = (field[0, 2:, 1:-1, :] - field[0, :-2, 1:-1, :]) + (field[1, 1:-1, 2:, :] - field[1, 1:-1, :-2, :])
    summed = summed + (jnp.roll(middle, -1, -1) - jnp.roll(middle, 1, -1))
    return summed / (2.0 * spacing)


def velocity_update(velo_rim, press_rim, solid_share, force_part, spacing):
    middle = trim_plane(velo_rim, 1)
    damping = penalty * solid_share
    diagonal = 6.0 * viscosity / (spacing * spacing) + damping
    residual = force_part - gradient(press_rim, spacing) + viscosity * laplace(velo_rim, spacing) - damping * middle
    return middle + relaxation * residual / diagonal


def block_mean(field):
    leading = field.shape[:-3]
    sizes_a, sizes_b, sizes_c = field.shape[-3:]
    shaped = field.reshape(leading + (sizes_a // 4, 4, sizes_b // 4, 4, sizes_c // 4, 4))
    return shaped.mean(axis=(-5, -3, -1))


def interpolation(fine_len, coarse_len, fine_offset, coarse_offset, period):
    fine_rows = lax.broadcasted_iota(jnp.int32, (fine_len, coarse_len), 0) + fine_offset
    coarse_cols = lax.broadcasted_iota(jnp.int32, (fine_len, coarse_len), 1) + coarse_offset
    lower_index = (fine_rows - 2) // 4
    fraction = ((fine_rows + 2) % 4).astype(jnp.float32) * 0.25 + 0.125
    if period > 0:
        first_hit = (lower_index - coarse_cols) % period == 0
        second_hit = (lower_index + 1 - coarse_cols) % period == 0
    else:
        first_hit = lower_index == coarse_cols
        second_hit = lower_index + 1 == coarse_cols
    return jnp.where(first_hit, 1.0 - fraction, 0.0) + jnp.where(second_hit, fraction, 0.0)


def wrapped(field):
    return jnp.pad(field, [(0, 0)] * (field.ndim - 3) + [(1, 1), (1, 1), (0, 0)], mode="wrap")


def periodic_sweep(velo_now, press_now, solid_share, force_part, spacing):
    new_velocity = velocity_update(wrapped(velo_now), wrapped(press_now), solid_share, force_part, spacing)
    new_pressure = press_now - pressure_step * divergence(wrapped(new_velocity), spacing)
    return new_velocity, new_pressure


def reference(solid_mask, forcing):
    solid_share = solid_mask.astype(jnp.float32)
    drive_vector = jnp.array([mean_drive, 0.0, 0.0], dtype=jnp.float32).reshape(3, 1, 1, 1)
    force_all = forcing + drive_vector
    coarse_chi = block_mean(solid_share)
    coarse_force = block_mean(force_all)
    velo_now = jnp.zeros((3,) + coarse_chi.shape, jnp.float32)
    press_now = jnp.zeros(coarse_chi.shape, jnp.float32)
    for number in range(2):
        velo_now, press_now = periodic_sweep(velo_now, press_now, coarse_chi, coarse_force, 4.0)
    stacked = jnp.concatenate([velo_now, press_now[None]], 0)
    size_x, size_y, size_z = solid_mask.shape
    coarse_x, coarse_y, coarse_z = coarse_chi.shape
    along_z = interpolation(size_z, coarse_z, 0, 0, coarse_z)
    along_y = interpolation(size_y, coarse_y, 0, 0, coarse_y)
    along_x = interpolation(size_x, coarse_x, 0, 0, coarse_x)
    stacked = jnp.einsum("fabk,zk->fabz", stacked, along_z, precision=lax.Precision.HIGHEST)
    stacked = jnp.einsum("fakz,bk->fabz", stacked, along_y, precision=lax.Precision.HIGHEST)
    stacked = jnp.einsum("fkbz,ak->fabz", stacked, along_x, precision=lax.Precision.HIGHEST)
    velo_now, press_now = stacked[:3], stacked[3]
    for number in range(2):
        velo_now, press_now = periodic_sweep(velo_now, press_now, solid_share, force_all, 1.0)
    return velo_now, press_now
```

```python
import functools

import jax
import jax.numpy as jnp
from jax import lax
from jax.experimental import pallas as pl
from jax.experimental.pallas import tpu as pltpu
from jax.sharding import PartitionSpec as P

viscosity = 1.0
penalty = 10.0
relaxation = 0.8
pressure_step = 1.0
mean_drive = 1.0

keep = 1.0 - relaxation
pore_step = relaxation / (6.0 * viscosity)
solid_step = relaxation / (6.0 * viscosity + penalty)

x_depths = ((0, 3), (1, 2), (2, 2), (3, 3))
y_depths = ((0, 2), (1, 3), (2, 2), (3, 3))
corner_cells = ((0, 1, 1), (0, 1, 2), (1, 1, 1), (1, 2, 1), (3, 1, 1), (3, 1, 2), (3, 2, 1))


def roll(value, shift):
    return pltpu.roll(value, shift % value.shape[-1], value.ndim - 1)


def lane_phase(shape):
    return lax.broadcasted_iota(jnp.int32, shape, len(shape) - 1) % 4


def step_of(mask):
    return jnp.where(mask != 0, solid_step, pore_step).astype(jnp.float32)


def pack_kernel(sizes, mask_ref, force_ref, mp_ref, mm_ref, xp_ref, xm_ref, yp_ref, ym_ref, sums):
    X, Y, Z = sizes
    cx, cy = X // 4, Y // 4

    def rows(field, index):
        if field == 3:
            return mask_ref[index, :]
        base = field * X * Y
        moved = pl.ds(base + index.start, index.size, index.stride)
        return force_ref[moved, :]

    def values(field, start, size, stride=1):
        taken = rows(field, pl.ds(start, size, stride))
        return step_of(taken) if field == 3 else taken

    phase = lane_phase((cy, Z))
    means = []
    for field in range(4):
        for block in range(cx):
            total = None
            for plane in range(4):
                part = rows(field, pl.ds((4 * block + plane) * Y, Y)).astype(jnp.float32)
                total = part if total is None else total + part
            sums[field, block] = total
    for block in range(cx):
        packed = None
        for field in range(4):
            total = sums[field, block, pl.ds(0, cy, 4), :]
            for row in range(1, 4):
                total = total + sums[field, block, pl.ds(row, cy, 4), :]
            total = total + jnp.where(phase % 2 == 0, roll(total, -1), roll(total, 1))
            total = total + jnp.where(phase < 2, roll(total, -2), roll(total, 2))
            mean = total * (1.0 / 64.0)
            if field == 0:
                mean = mean + mean_drive
            packed = mean if packed is None else jnp.where(phase == field, mean, packed)
        mp_ref[block] = packed
        mm_ref[block] = packed
    for ref, high in ((mp_ref, True), (mm_ref, False)):
        for top in (True, False):
            for number, (field, dx, dy) in enumerate(corner_cells):
                x = X - dx if high else dx - 1
                y = Y - dy if top else dy - 1
                ref[cx + (0 if top else 1), pl.ds(number, 1), :] = values(field, x * Y + y, 1)
            ref[cx + (0 if top else 1), pl.ds(7, 1), :] = jnp.zeros((1, Z), jnp.float32)
    for ref, high in ((xp_ref, True), (xm_ref, False)):
        number = 0
        for field, depth in x_depths:
            for plane in range(depth):
                x = X - depth + plane if high else plane
                ref[number] = values(field, x * Y, Y)
                number += 1
    for ref, high in ((yp_ref, True), (ym_ref, False)):
        number = 0
        for field, depth in y_depths:
            for row in range(depth):
                y = Y - depth + row if high else row
                ref[number] = values(field, y, X, Y)
                number += 1


def solve_kernel(sizes, *refs):
    X, Y, Z = sizes
    cx, cy = X // 4, Y // 4
    coarse_in = refs[:9]
    xl_ref, xr_ref, yd_ref, yu_ref, mask_ref, force_ref = refs[9:15]
    velo_out, press_out = refs[15:17]
    (cpk, corners, cforce, cstep, cvel, cvel2, cpress, cfine, yfine, force, step, mask, yd, yu, state, mid, sems) = refs[17:]
    ex, ey, fy = 4, 16, 8

    copies = []

    def copy(src, dst):
        made = pltpu.make_async_copy(src, dst, sems.at[len(copies)])
        made.start()
        copies.append(made)
        return made

    first = []
    for a in range(3):
        for b in range(3):
            first.append(copy(coarse_in[3 * a + b].at[pl.ds(0, cx)], cpk.at[pl.ds(a * cx, cx), pl.ds(b * cy, cy), :]))
    second = []
    for number, (a, b) in enumerate(((0, 0), (0, 2), (2, 0), (2, 2))):
        second.append(copy(coarse_in[3 * a + b].at[cx + (0 if b == 0 else 1)], corners.at[number]))
    second.append(copy(yd_ref, yd))
    second.append(copy(yu_ref, yu))
    second.append(copy(mask_ref, mask))
    for field in range(3):
        second.append(copy(force_ref.at[field], force.at[field, pl.ds(ex, X), pl.ds(fy, Y), :]))
    for ref, high in ((xl_ref, False), (xr_ref, True)):
        number = 0
        for field, depth in x_depths:
            x = ex + X if high else ex - depth
            target = step.at[pl.ds(x, depth), pl.ds(fy, Y), :] if field == 3 else force.at[field, pl.ds(x, depth), pl.ds(fy, Y), :]
            second.append(copy(ref.at[pl.ds(number, depth)], target))
            number += depth

    for made in first:
        made.wait()

    tall = 3 * cy
    mid_rows, up_rows, down_rows = pl.ds(cy, tall), pl.ds(cy + 1, tall), pl.ds(cy - 1, tall)
    phase = lane_phase((tall, Z))
    for x in range(3 * cx):
        packed = cpk[x]
        moved = {k: (packed if k == 0 else roll(packed, k)) for k in range(-3, 4)}
        spread = []
        for field in range(4):
            value = moved[3 - field]
            for t in range(3):
                value = jnp.where(phase == t, moved[t - field], value)
            spread.append(value)
        ratio = relaxation / (6.0 * viscosity / 16.0 + penalty * spread[3])
        cstep[x] = ratio
        for a in range(3):
            cforce[a, x] = spread[a]
            cvel[a, x, mid_rows, :] = ratio * spread[a]

    def coarse_div(vel, x):
        along_z = vel[2, x, mid_rows, :]
        total = (vel[0, x + 1, mid_rows, :] - vel[0, x - 1, mid_rows, :]) + (vel[1, x, up_rows, :] - vel[1, x, down_rows, :])
        return (total + (roll(along_z, -4) - roll(along_z, 4))) * 0.125

    for x in range(2, 3 * cx - 2):
        cpress[x, mid_rows, :] = -pressure_step * coarse_div(cvel, x)
    for x in range(3, 3 * cx - 3):
        ratio = cstep[x]
        press = cpress[x, mid_rows, :]
        slopes = (
            cpress[x + 1, mid_rows, :] - cpress[x - 1, mid_rows, :],
            cpress[x, up_rows, :] - cpress[x, down_rows, :],
            roll(press, -4) - roll(press, 4),
        )
        for a in range(3):
            middle = cvel[a, x, mid_rows, :]
            near = cvel[a, x + 1, mid_rows, :] + cvel[a, x - 1, mid_rows, :]
            near = near + (cvel[a, x, up_rows, :] + cvel[a, x, down_rows, :])
            near = near + (roll(middle, 4) + roll(middle, -4))
            source = cforce[a, x] - 0.125 * slopes[a] + (viscosity / 16.0) * near
            cvel2[a, x, mid_rows, :] = keep * middle + ratio * source
    weight = phase.astype(jnp.float32)
    weight = ((phase + 2) % 4).astype(jnp.float32) * 0.25 + 0.125

    def stretch_z(value):
        return (1.0 - weight) * roll(value, 2) + weight * roll(value, -2)

    for number in range(cx + 4):
        x = number + cx - 2
        press = cpress[x, mid_rows, :] - pressure_step * coarse_div(cvel2, x)
        cfine[3, number] = stretch_z(press)
        for a in range(3):
            cfine[a, number] = stretch_z(cvel2[a, x, mid_rows, :])
    count = cy + 4
    for field in range(4):
        for x in range(cx + 4):
            low = cfine[field, x, pl.ds(cy - 3, count), :]
            here = cfine[field, x, pl.ds(cy - 2, count), :]
            high = cfine[field, x, pl.ds(cy - 1, count), :]
            yfine[field, x, pl.ds(0, count, 4), :] = 0.375 * low + 0.625 * here
            yfine[field, x, pl.ds(1, count, 4), :] = 0.125 * low + 0.875 * here
            yfine[field, x, pl.ds(2, count, 4), :] = 0.875 * here + 0.125 * high
            yfine[field, x, pl.ds(3, count, 4), :] = 0.625 * here + 0.375 * high

    wide = Y + 16
    wide_rows = pl.ds(ey - 8, wide)

    def stretch_x(m, carry):
        for field in range(4):
            low, here, high = yfine[field, m], yfine[field, m + 1], yfine[field, m + 2]
            state[field, 4 * m, wide_rows, :] = 0.375 * low + 0.625 * here
            state[field, 4 * m + 1, wide_rows, :] = 0.125 * low + 0.875 * here
            state[field, 4 * m + 2, wide_rows, :] = 0.875 * here + 0.125 * high
            state[field, 4 * m + 3, wide_rows, :] = 0.625 * here + 0.375 * high
        return carry

    lax.fori_loop(0, cx + 2, stretch_x, 0)

    for made in second:
        made.wait()
    for x in range(X):
        step[ex + x, pl.ds(fy, Y), :] = step_of(mask[x])
    for ref, high in ((yd, False), (yu, True)):
        number = 0
        for field, depth in y_depths:
            for row in range(depth):
                y = fy + Y + row if high else fy - depth + row
                for x in range(X):
                    line = ref[number, pl.ds(x, 1), :]
                    if field == 3:
                        step[ex + x, pl.ds(y, 1), :] = line
                    else:
                        force[field, ex + x, pl.ds(y, 1), :] = line
                number += 1
    for number, (a, b) in enumerate(((0, 0), (0, 2), (2, 0), (2, 2))):
        for row, (field, dx, dy) in enumerate(corner_cells):
            x = ex - dx if a == 0 else ex + X - 1 + dx
            y = fy - dy if b == 0 else fy + Y - 1 + dy
            line = corners[number, pl.ds(row, 1), :]
            if field == 3:
                step[x, pl.ds(y, 1), :] = line
            else:
                force[field, x, pl.ds(y, 1), :] = line

    def move(old, new, x, components, start, size):
        rows, above, below = pl.ds(ey + start, size), pl.ds(ey + start + 1, size), pl.ds(ey + start - 1, size)
        source_rows = pl.ds(fy + start, size)
        ratio = step[x, source_rows, :]
        for a in components:
            if a == 0:
                slope = state[3, x + 1, rows, :] - state[3, x - 1, rows, :]
            elif a == 1:
                slope = state[3, x, above, :] - state[3, x, below, :]
            else:
                press = state[3, x, rows, :]
                slope = roll(press, -1) - roll(press, 1)
            middle = old[a, x, rows, :]
            near = old[a, x + 1, rows, :] + old[a, x - 1, rows, :]
            near = near + (old[a, x, above, :] + old[a, x, below, :])
            near = near + (roll(middle, 1) + roll(middle, -1))
            source = force[a, x, source_rows, :]
            if a == 0:
                source = source + mean_drive
            source = source - 0.5 * slope + near
            new[a, x, rows, :] = keep * middle + ratio * source

    def divergence(vel, x, start, size):
        rows, above, below = pl.ds(ey + start, size), pl.ds(ey + start + 1, size), pl.ds(ey + start - 1, size)
        along_z = vel[2, x, rows, :]
        total = (vel[0, x + 1, rows, :] - vel[0, x - 1, rows, :]) + (vel[1, x, above, :] - vel[1, x, below, :])
        return (total + (roll(along_z, -1) - roll(along_z, 1))) * (0.5 * pressure_step)

    def loop(low, high, body):
        def run(x, carry):
            body(x)
            return carry

        lax.fori_loop(low, high, run, 0)

    loop(1, X + 7, lambda x: move(state, mid, x, (0, 1, 2), -8, wide))

    def press_first(x):
        state[3, x, wide_rows, :] = state[3, x, wide_rows, :] - divergence(mid, x, -8, wide)

    loop(2, X + 6, press_first)
    move(mid, state, ex - 1, (0,), 0, Y)
    move(mid, state, ex + X, (0,), 0, Y)

    def second_move(x):
        move(mid, state, x, (0, 2), 0, Y)
        move(mid, state, x, (1,), -8, wide)

    loop(ex, ex + X, second_move)
    inner = pl.ds(ey, Y)
    last = [copy(state.at[a, pl.ds(ex, X), inner, :], velo_out.at[a]) for a in range(3)]

    def press_second(x):
        mask_rows = state[3, x, inner, :] - divergence(state, x, 0, Y)
        step[x, pl.ds(fy, Y), :] = mask_rows

    loop(ex, ex + X, press_second)
    last.append(copy(step.at[pl.ds(ex, X), pl.ds(fy, Y), :], press_out))
    for made in last:
        made.wait()


def shift(value, axis, by):
    count = lax.axis_size(axis)
    return lax.ppermute(value, axis, [(i, (i + by) % count) for i in range(count)])


def shards(solid_mask, forcing):
    X, Y, Z = sizes = solid_mask.shape
    cx, cy = X // 4, Y // 4
    f32 = jnp.float32
    made = jax.ShapeDtypeStruct
    message = made((cx + 2, 8, Z), f32)
    planes = made((10, Y, Z), f32)
    lines = made((10, X, Z), f32)
    mp, mm, xp, xm, yp, ym = pl.pallas_call(
        functools.partial(pack_kernel, sizes),
        out_shape=(message, message, planes, planes, lines, lines),
        scratch_shapes=[pltpu.VMEM((4, cx, Y, Z), f32)],
        compiler_params=pltpu.CompilerParams(vmem_limit_bytes=40 * 2**20),
        name="pack",
    )(solid_mask.reshape(X * Y, Z), forcing.reshape(3 * X * Y, Z))
    ml = shift(mp, "grp", 1)
    mr = shift(mm, "grp", -1)
    xl = shift(xp, "grp", 1)
    xr = shift(xm, "grp", -1)
    own = (ml, mp, mr)
    up = [shift(value, "dev", -1) for value in own]
    down = [shift(value, "dev", 1) for value in own]
    yu = shift(ym, "dev", -1)
    yd = shift(yp, "dev", 1)
    blocks = []
    for a in range(3):
        blocks += [down[a], own[a], up[a]]
    anywhere = pl.BlockSpec(memory_space=pl.ANY)
    tall = 3 * cy
    vmem = pltpu.VMEM
    return pl.pallas_call(
        functools.partial(solve_kernel, sizes),
        out_shape=(made((3, X, Y, Z), f32), made((X, Y, Z), f32)),
        in_specs=[anywhere] * 15,
        out_specs=(anywhere, anywhere),
        scratch_shapes=[
            vmem((3 * cx, tall, Z), f32),
            vmem((4, 8, Z), f32),
            vmem((3, 3 * cx, tall, Z), f32),
            vmem((3 * cx, tall, Z), f32),
            vmem((3, 3 * cx, tall + 2 * cy, Z), f32),
            vmem((3, 3 * cx, tall + 2 * cy, Z), f32),
            vmem((3 * cx, tall + 2 * cy, Z), f32),
            vmem((4, cx + 4, tall, Z), f32),
            vmem((4, cx + 4, Y + 16, Z), f32),
            vmem((3, X + 8, Y + 16, Z), f32),
            vmem((X + 8, Y + 16, Z), f32),
            vmem((X, Y, Z), jnp.int32),
            vmem((10, X, Z), f32),
            vmem((10, X, Z), f32),
            vmem((4, X + 8, Y + 32, Z), f32),
            vmem((3, X + 8, Y + 32, Z), f32),
            pltpu.SemaphoreType.DMA((40,)),
        ],
        compiler_params=pltpu.CompilerParams(vmem_limit_bytes=56 * 2**20),
        name="solve",
    )(*blocks, xl, xr, yd, yu, solid_mask, forcing)


def solution(mesh):
    in_specs = (P("grp", "dev", None), P(None, "grp", "dev", None))
    out_specs = (P(None, "grp", "dev", None), P("grp", "dev", None))
    return jax.shard_map(shards, mesh=mesh, in_specs=in_specs, out_specs=out_specs, check_vma=False)
```

```python
import functools

import jax
import jax.numpy as jnp
from jax import lax
from jax.experimental import pallas as pl
from jax.experimental.pallas import tpu as pltpu
from jax.sharding import PartitionSpec as P

viscosity = 1.0
penalty = 10.0
relaxation = 0.8
pressure_step = 1.0
mean_drive = 1.0

keep = 1.0 - relaxation
pore_step = relaxation / (6.0 * viscosity)
solid_step = relaxation / (6.0 * viscosity + penalty)

x_depths = ((0, 3), (1, 2), (2, 2), (3, 3))
y_depths = ((0, 2), (1, 3), (2, 2), (3, 3))
corner_cells = ((0, 1, 1), (0, 1, 2), (1, 1, 1), (1, 2, 1), (3, 1, 1), (3, 1, 2), (3, 2, 1))


def roll(value, shift):
    return pltpu.roll(value, shift % value.shape[-1], value.ndim - 1)


def lane_phase(shape):
    return lax.broadcasted_iota(jnp.int32, shape, len(shape) - 1) % 4


def step_of(mask):
    return jnp.where(mask != 0, solid_step, pore_step).astype(jnp.float32)


def pack_kernel(sizes, mask_in, force_in, mp_ref, mm_ref, xp_ref, xm_ref, yp_ref, ym_ref, mask_ref, force_ref, sums, sems):
    X, Y, Z = sizes
    cx, cy = X // 4, Y // 4
    copies = [
        pltpu.make_async_copy(mask_in, mask_ref, sems.at[3]),
    ]
    for field in range(3):
        part = pl.ds(field * X * Y, X * Y)
        copies.append(pltpu.make_async_copy(force_in.at[part], force_ref.at[part], sems.at[field]))
    for made in copies:
        made.start()
    for made in copies:
        made.wait()

    def rows(field, index):
        if field == 3:
            return mask_ref[index, :]
        base = field * X * Y
        moved = pl.ds(base + index.start, index.size, index.stride)
        return force_ref[moved, :]

    def values(field, start, size, stride=1):
        taken = rows(field, pl.ds(start, size, stride))
        return step_of(taken) if field == 3 else taken

    phase = lane_phase((cy, Z))
    means = []
    for field in range(4):
        for block in range(cx):
            total = None
            for plane in range(4):
                part = rows(field, pl.ds((4 * block + plane) * Y, Y)).astype(jnp.float32)
                total = part if total is None else total + part
            sums[field, block] = total
    for block in range(cx):
        packed = None
        for field in range(4):
            total = sums[field, block, pl.ds(0, cy, 4), :]
            for row in range(1, 4):
                total = total + sums[field, block, pl.ds(row, cy, 4), :]
            total = total + jnp.where(phase % 2 == 0, roll(total, -1), roll(total, 1))
            total = total + jnp.where(phase < 2, roll(total, -2), roll(total, 2))
            mean = total * (1.0 / 64.0)
            if field == 0:
                mean = mean + mean_drive
            packed = mean if packed is None else jnp.where(phase == field, mean, packed)
        mp_ref[block] = packed
        mm_ref[block] = packed
    for ref, high in ((mp_ref, True), (mm_ref, False)):
        for top in (True, False):
            for number, (field, dx, dy) in enumerate(corner_cells):
                x = X - dx if high else dx - 1
                y = Y - dy if top else dy - 1
                ref[cx + (0 if top else 1), pl.ds(number, 1), :] = values(field, x * Y + y, 1)
            ref[cx + (0 if top else 1), pl.ds(7, 1), :] = jnp.zeros((1, Z), jnp.float32)
    for ref, high in ((xp_ref, True), (xm_ref, False)):
        number = 0
        for field, depth in x_depths:
            for plane in range(depth):
                x = X - depth + plane if high else plane
                ref[number] = values(field, x * Y, Y)
                number += 1
    for ref, high in ((yp_ref, True), (ym_ref, False)):
        number = 0
        for field, depth in y_depths:
            for row in range(depth):
                y = Y - depth + row if high else row
                line = values(field, y, X, Y)
                for tile in range(X // 8):
                    ref[number * (X // 8) + tile] = line[8 * tile : 8 * tile + 8]
                number += 1


def solve_kernel(sizes, *refs):
    X, Y, Z = sizes
    cx, cy = X // 4, Y // 4
    down_ref, up_ref, ml_ref, mp_ref, mr_ref, xl_ref, xr_ref, mask, force_ref = refs[:9]
    velo_out, press_out = refs[9:11]
    (cforce, cstep, cvel, cvel2, cpress, cfine, yfine, force, step, state, mid, sems) = refs[11:]
    ex, ey, fy = 4, 16, 8

    copies = []

    def copy(src, dst):
        made = pltpu.make_async_copy(src, dst, sems.at[len(copies)])
        made.start()
        copies.append(made)
        return made

    second = []
    for field in range(3):
        second.append(copy(force_ref.at[field], force.at[field, pl.ds(ex, X), pl.ds(fy, Y), :]))
    for ref, high in ((xl_ref, False), (xr_ref, True)):
        number = 0
        for field, depth in x_depths:
            x = ex + X if high else ex - depth
            target = step.at[pl.ds(x, depth), pl.ds(fy, Y), :] if field == 3 else force.at[field, pl.ds(x, depth), pl.ds(fy, Y), :]
            second.append(copy(ref.at[pl.ds(number, depth)], target))
            number += depth

    tall = 3 * cy
    mid_rows, up_rows, down_rows = pl.ds(cy, tall), pl.ds(cy + 1, tall), pl.ds(cy - 1, tall)
    phase = lane_phase((tall, Z))
    for x in range(3 * cx):
        middle_ref = (ml_ref, mp_ref, mr_ref)[x // cx]
        packed = jnp.concatenate([down_ref[x], middle_ref[x % cx], up_ref[x]], 0)
        moved = {k: (packed if k == 0 else roll(packed, k)) for k in range(-3, 4)}
        spread = []
        for field in range(4):
            value = moved[3 - field]
            for t in range(3):
                value = jnp.where(phase == t, moved[t - field], value)
            spread.append(value)
        ratio = relaxation / (6.0 * viscosity / 16.0 + penalty * spread[3])
        cstep[x] = ratio
        for a in range(3):
            cforce[a, x] = spread[a]
            cvel[a, x, mid_rows, :] = ratio * spread[a]

    def coarse_div(vel, x):
        along_z = vel[2, x, mid_rows, :]
        total = (vel[0, x + 1, mid_rows, :] - vel[0, x - 1, mid_rows, :]) + (vel[1, x, up_rows, :] - vel[1, x, down_rows, :])
        return (total + (roll(along_z, -4) - roll(along_z, 4))) * 0.125

    for x in range(2, 3 * cx - 2):
        cpress[x, mid_rows, :] = -pressure_step * coarse_div(cvel, x)
    for x in range(3, 3 * cx - 3):
        ratio = cstep[x]
        press = cpress[x, mid_rows, :]
        slopes = (
            cpress[x + 1, mid_rows, :] - cpress[x - 1, mid_rows, :],
            cpress[x, up_rows, :] - cpress[x, down_rows, :],
            roll(press, -4) - roll(press, 4),
        )
        for a in range(3):
            middle = cvel[a, x, mid_rows, :]
            near = cvel[a, x + 1, mid_rows, :] + cvel[a, x - 1, mid_rows, :]
            near = near + (cvel[a, x, up_rows, :] + cvel[a, x, down_rows, :])
            near = near + (roll(middle, 4) + roll(middle, -4))
            source = cforce[a, x] - 0.125 * slopes[a] + (viscosity / 16.0) * near
            cvel2[a, x, mid_rows, :] = keep * middle + ratio * source
    weight = phase.astype(jnp.float32)
    weight = ((phase + 2) % 4).astype(jnp.float32) * 0.25 + 0.125

    def stretch_z(value):
        return (1.0 - weight) * roll(value, 2) + weight * roll(value, -2)

    for number in range(cx + 4):
        x = number + cx - 2
        press = cpress[x, mid_rows, :] - pressure_step * coarse_div(cvel2, x)
        cfine[3, number] = stretch_z(press)
        for a in range(3):
            cfine[a, number] = stretch_z(cvel2[a, x, mid_rows, :])
    count = cy + 4
    for field in range(4):
        for x in range(cx + 4):
            low = cfine[field, x, pl.ds(cy - 3, count), :]
            here = cfine[field, x, pl.ds(cy - 2, count), :]
            high = cfine[field, x, pl.ds(cy - 1, count), :]
            yfine[field, x, pl.ds(0, count, 4), :] = 0.375 * low + 0.625 * here
            yfine[field, x, pl.ds(1, count, 4), :] = 0.125 * low + 0.875 * here
            yfine[field, x, pl.ds(2, count, 4), :] = 0.875 * here + 0.125 * high
            yfine[field, x, pl.ds(3, count, 4), :] = 0.625 * here + 0.375 * high

    wide = Y + 16
    wide_rows = pl.ds(ey - 8, wide)

    def stretch_x(m, carry):
        for field in range(4):
            low, here, high = yfine[field, m], yfine[field, m + 1], yfine[field, m + 2]
            state[field, 4 * m, wide_rows, :] = 0.375 * low + 0.625 * here
            state[field, 4 * m + 1, wide_rows, :] = 0.125 * low + 0.875 * here
            state[field, 4 * m + 2, wide_rows, :] = 0.875 * here + 0.125 * high
            state[field, 4 * m + 3, wide_rows, :] = 0.625 * here + 0.375 * high
        return carry

    lax.fori_loop(0, cx + 2, stretch_x, 0)

    for made in second:
        made.wait()
    for x in range(X):
        step[ex + x, pl.ds(fy, Y), :] = step_of(mask[x])
    for ref, high in ((down_ref, False), (up_ref, True)):
        number = 0
        for field, depth in y_depths:
            for row in range(depth):
                y = fy + Y + row if high else fy - depth + row
                for x in range(X):
                    place = number * X + x
                    line = ref[3 * cx + 2 + place // 8, pl.ds(place % 8, 1), :]
                    if field == 3:
                        step[ex + x, pl.ds(y, 1), :] = line
                    else:
                        force[field, ex + x, pl.ds(y, 1), :] = line
                number += 1
        for side in range(2):
            for row, (field, dx, dy) in enumerate(corner_cells):
                x = ex - dx if side == 0 else ex + X - 1 + dx
                y = fy + Y - 1 + dy if high else fy - dy
                line = ref[3 * cx + side, pl.ds(row, 1), :]
                if field == 3:
                    step[x, pl.ds(y, 1), :] = line
                else:
                    force[field, x, pl.ds(y, 1), :] = line

    def move(old, new, x, components, start, size):
        rows, above, below = pl.ds(ey + start, size), pl.ds(ey + start + 1, size), pl.ds(ey + start - 1, size)
        source_rows = pl.ds(fy + start, size)
        ratio = step[x, source_rows, :]
        for a in components:
            if a == 0:
                slope = state[3, x + 1, rows, :] - state[3, x - 1, rows, :]
            elif a == 1:
                slope = state[3, x, above, :] - state[3, x, below, :]
            else:
                press = state[3, x, rows, :]
                slope = roll(press, -1) - roll(press, 1)
            middle = old[a, x, rows, :]
            near = old[a, x + 1, rows, :] + old[a, x - 1, rows, :]
            near = near + (old[a, x, above, :] + old[a, x, below, :])
            near = near + (roll(middle, 1) + roll(middle, -1))
            source = force[a, x, source_rows, :]
            if a == 0:
                source = source + mean_drive
            source = source - 0.5 * slope + near
            new[a, x, rows, :] = keep * middle + ratio * source

    def divergence(vel, x, start, size):
        rows, above, below = pl.ds(ey + start, size), pl.ds(ey + start + 1, size), pl.ds(ey + start - 1, size)
        along_z = vel[2, x, rows, :]
        total = (vel[0, x + 1, rows, :] - vel[0, x - 1, rows, :]) + (vel[1, x, above, :] - vel[1, x, below, :])
        return (total + (roll(along_z, -1) - roll(along_z, 1))) * (0.5 * pressure_step)

    def loop(low, high, body):
        def run(x, carry):
            body(x)
            return carry

        lax.fori_loop(low, high, run, 0, unroll=10)

    loop(1, X + 7, lambda x: move(state, mid, x, (0, 1, 2), -8, wide))

    def press_first(x):
        state[3, x, wide_rows, :] = state[3, x, wide_rows, :] - divergence(mid, x, -8, wide)

    loop(2, X + 6, press_first)
    move(mid, state, ex - 1, (0,), 0, Y)
    move(mid, state, ex + X, (0,), 0, Y)

    def second_move(x):
        move(mid, state, x, (0, 2), 0, Y)
        move(mid, state, x, (1,), -8, wide)

    loop(ex, ex + X, second_move)
    inner = pl.ds(ey, Y)
    last = [copy(state.at[a, pl.ds(ex, X), inner, :], velo_out.at[a]) for a in range(3)]

    def press_second(x):
        mask_rows = state[3, x, inner, :] - divergence(state, x, 0, Y)
        step[x, pl.ds(fy, Y), :] = mask_rows

    loop(ex, ex + X, press_second)
    last.append(copy(step.at[pl.ds(ex, X), pl.ds(fy, Y), :], press_out))
    for made in last:
        made.wait()


def relay_kernel(sizes, ml_ref, mp_ref, mr_ref, yp_ref, ym_ref, up_ref, down_ref):
    X, Y, Z = sizes
    cx = X // 4
    for ref, lines, corner in ((down_ref, yp_ref, cx), (up_ref, ym_ref, cx + 1)):
        for number, source in enumerate((ml_ref, mp_ref, mr_ref)):
            ref[pl.ds(number * cx, cx)] = source[pl.ds(0, cx)]
        ref[3 * cx] = ml_ref[corner]
        ref[3 * cx + 1] = mr_ref[corner]
        ref[pl.ds(3 * cx + 2, 10 * X // 8)] = lines[...]


def shift(value, axis, by):
    count = lax.axis_size(axis)
    return lax.ppermute(value, axis, [(i, (i + by) % count) for i in range(count)])


def shards(solid_mask, forcing):
    X, Y, Z = sizes = solid_mask.shape
    cx, cy = X // 4, Y // 4
    f32 = jnp.float32
    made = jax.ShapeDtypeStruct
    vmem = pltpu.VMEM
    anywhere = pl.BlockSpec(memory_space=pl.ANY)
    near = pl.BlockSpec(memory_space=vmem)
    message = made((cx + 2, 8, Z), f32)
    planes = made((10, Y, Z), f32)
    lines = made((10 * X // 8, 8, Z), f32)
    mp, mm, xp, xm, yp, ym, mask, force = pl.pallas_call(
        functools.partial(pack_kernel, sizes),
        out_shape=(message, message, planes, planes, lines, lines, made((X * Y, Z), jnp.int32), made((3 * X * Y, Z), f32)),
        in_specs=[pl.BlockSpec(memory_space=pltpu.HBM)] * 2,
        out_specs=[near] * 8,
        scratch_shapes=[vmem((4, cx, Y, Z), f32), pltpu.SemaphoreType.DMA((4,))],
        compiler_params=pltpu.CompilerParams(vmem_limit_bytes=12 * 2**20),
        name="pack",
    )(
        pltpu.with_memory_space_constraint(solid_mask.reshape(X * Y, Z), pltpu.HBM),
        pltpu.with_memory_space_constraint(forcing.reshape(3 * X * Y, Z), pltpu.HBM),
    )
    xl = shift(xp, "grp", 1)
    xr = shift(xm, "grp", -1)
    ml = shift(mp, "grp", 1)
    mr = shift(mm, "grp", -1)
    joined = made((3 * cx + 2 + 10 * X // 8, 8, Z), f32)
    to_up, to_down = pl.pallas_call(
        functools.partial(relay_kernel, sizes),
        out_shape=(joined, joined),
        in_specs=[near] * 5,
        out_specs=[near] * 2,
        compiler_params=pltpu.CompilerParams(vmem_limit_bytes=2 * 2**20),
        name="relay",
    )(ml, mp, mr, yp, ym)
    up = shift(to_up, "dev", -1)
    down = shift(to_down, "dev", 1)
    tall = 3 * cy
    return pl.pallas_call(
        functools.partial(solve_kernel, sizes),
        out_shape=(made((3, X, Y, Z), f32), made((X, Y, Z), f32)),
        in_specs=[near] * 9,
        out_specs=(anywhere, anywhere),
        scratch_shapes=[
            vmem((3, 3 * cx, tall, Z), f32),
            vmem((3 * cx, tall, Z), f32),
            vmem((3, 3 * cx, tall + 2 * cy, Z), f32),
            vmem((3, 3 * cx, tall + 2 * cy, Z), f32),
            vmem((3 * cx, tall + 2 * cy, Z), f32),
            vmem((4, cx + 4, tall, Z), f32),
            vmem((4, cx + 4, Y + 16, Z), f32),
            vmem((3, X + 8, Y + 16, Z), f32),
            vmem((X + 8, Y + 16, Z), f32),
            vmem((4, X + 8, Y + 32, Z), f32),
            vmem((3, X + 8, Y + 32, Z), f32),
            pltpu.SemaphoreType.DMA((20,)),
        ],
        compiler_params=pltpu.CompilerParams(vmem_limit_bytes=32 * 2**20),
        name="solve",
    )(down, up, ml, mp, mr, xl, xr, mask.reshape(X, Y, Z), force.reshape(3, X, Y, Z))


def solution(mesh):
    in_specs = (P("grp", "dev", None), P(None, "grp", "dev", None))
    out_specs = (P(None, "grp", "dev", None), P("grp", "dev", None))
    return jax.shard_map(shards, mesh=mesh, in_specs=in_specs, out_specs=out_specs, check_vma=False)
```

```python
import functools

import jax
import jax.numpy as jnp
from jax import lax
from jax.experimental import pallas as pl
from jax.experimental.pallas import tpu as pltpu
from jax.sharding import PartitionSpec as P

viscosity = 1.0
penalty = 10.0
relaxation = 0.8
pressure_step = 1.0
mean_drive = 1.0

keep = 1.0 - relaxation
pore_step = relaxation / (6.0 * viscosity)
solid_step = relaxation / (6.0 * viscosity + penalty)

x_depths = ((0, 3), (1, 2), (2, 2), (3, 3))
y_depths = ((0, 2), (1, 3), (2, 2), (3, 3))
corner_cells = ((0, 1, 1), (0, 1, 2), (1, 1, 1), (1, 2, 1), (3, 1, 1), (3, 1, 2), (3, 2, 1))


def roll(value, shift):
    return pltpu.roll(value, shift % value.shape[-1], value.ndim - 1)


def lane_phase(shape):
    return lax.broadcasted_iota(jnp.int32, shape, len(shape) - 1) % 4


def neighbour_matrices(Z, distance):
    source = lax.broadcasted_iota(jnp.int32, (2 * Z, Z), 0) % Z
    target = lax.broadcasted_iota(jnp.int32, (2 * Z, Z), 1)
    after = (source == (target + distance) % Z).astype(jnp.float32)
    before = (source == (target + Z - distance) % Z).astype(jnp.float32)
    return (after + before).astype(jnp.bfloat16), (after - before).astype(jnp.bfloat16)


def apply(matrix, values):
    high = values.astype(jnp.bfloat16)
    low = (values - high.astype(jnp.float32)).astype(jnp.bfloat16)
    return jnp.dot(jnp.concatenate([high, low], -1), matrix, preferred_element_type=jnp.float32)


def flat(values):
    return values.reshape(-1, values.shape[-1])


def step_of(mask):
    return jnp.where(mask != 0, solid_step, pore_step).astype(jnp.float32)


def pack_kernel(sizes, mask_in, force_in, mp_ref, mm_ref, xp_ref, xm_ref, yp_ref, ym_ref, mask_ref, force_ref, sums, sems):
    X, Y, Z = sizes
    cx, cy = X // 4, Y // 4
    copies = [
        pltpu.make_async_copy(mask_in, mask_ref, sems.at[3]),
    ]
    for field in range(3):
        part = pl.ds(field * X * Y, X * Y)
        copies.append(pltpu.make_async_copy(force_in.at[part], force_ref.at[part], sems.at[field]))
    for made in copies:
        made.start()
    for made in copies:
        made.wait()

    def rows(field, index):
        if field == 3:
            return mask_ref[index, :]
        base = field * X * Y
        moved = pl.ds(base + index.start, index.size, index.stride)
        return force_ref[moved, :]

    def values(field, start, size, stride=1):
        taken = rows(field, pl.ds(start, size, stride))
        return step_of(taken) if field == 3 else taken

    phase = lane_phase((cy, Z))
    means = []
    for field in range(4):
        for block in range(cx):
            total = None
            for plane in range(4):
                part = rows(field, pl.ds((4 * block + plane) * Y, Y)).astype(jnp.float32)
                total = part if total is None else total + part
            sums[field, block] = total
    for block in range(cx):
        packed = None
        for field in range(4):
            total = sums[field, block, pl.ds(0, cy, 4), :]
            for row in range(1, 4):
                total = total + sums[field, block, pl.ds(row, cy, 4), :]
            total = total + jnp.where(phase % 2 == 0, roll(total, -1), roll(total, 1))
            total = total + jnp.where(phase < 2, roll(total, -2), roll(total, 2))
            mean = total * (1.0 / 64.0)
            if field == 0:
                mean = mean + mean_drive
            packed = mean if packed is None else jnp.where(phase == field, mean, packed)
        mp_ref[block] = packed
        mm_ref[block] = packed
    for ref, high in ((mp_ref, True), (mm_ref, False)):
        for top in (True, False):
            for number, (field, dx, dy) in enumerate(corner_cells):
                x = X - dx if high else dx - 1
                y = Y - dy if top else dy - 1
                ref[cx + (0 if top else 1), pl.ds(number, 1), :] = values(field, x * Y + y, 1)
            ref[cx + (0 if top else 1), pl.ds(7, 1), :] = jnp.zeros((1, Z), jnp.float32)
    for ref, high in ((xp_ref, True), (xm_ref, False)):
        number = 0
        for field, depth in x_depths:
            for plane in range(depth):
                x = X - depth + plane if high else plane
                ref[number] = values(field, x * Y, Y)
                number += 1
    for ref, high in ((yp_ref, True), (ym_ref, False)):
        number = 0
        for field, depth in y_depths:
            for row in range(depth):
                y = Y - depth + row if high else row
                line = values(field, y, X, Y)
                for tile in range(X // 8):
                    ref[number * (X // 8) + tile] = line[8 * tile : 8 * tile + 8]
                number += 1


def coarse_kernel(sizes, down_ref, up_ref, ml_ref, mp_ref, mr_ref, yfine, cforce, cstep, cvel, cpress, cfine):
    X, Y, Z = sizes
    cx, cy = X // 4, Y // 4
    tall, deep = 3 * cy, cx + 10
    mid_rows, up_rows, down_rows = pl.ds(cy, tall), pl.ds(cy + 1, tall), pl.ds(cy - 1, tall)
    source = lax.broadcasted_iota(jnp.int32, (2 * Z, 4 * Z), 0) % Z
    target = lax.broadcasted_iota(jnp.int32, (2 * Z, 4 * Z), 1)
    spread = (source == (target % Z) // 4 * 4 + target // Z).astype(jnp.float32).astype(jnp.bfloat16)
    pair_sum, pair_gap = neighbour_matrices(Z, 4)
    source = lax.broadcasted_iota(jnp.int32, (2 * Z, Z), 0) % Z
    target = lax.broadcasted_iota(jnp.int32, (2 * Z, Z), 1)
    part = ((target + 2) % 4).astype(jnp.float32) * 0.25 + 0.125
    stretch = jnp.where(source == (target + Z - 2) % Z, 1.0 - part, 0.0) + jnp.where(source == (target + 2) % Z, part, 0.0)
    stretch = stretch.astype(jnp.bfloat16)

    packed = []
    for x in range(deep):
        number, plane = divmod(x + cx - 5, cx)
        packed += [down_ref[x], (ml_ref, mp_ref, mr_ref)[number][plane], up_ref[x]]
    fields = apply(spread, jnp.concatenate(packed, 0))
    shape = (deep, tall, Z)
    ratio = relaxation / (6.0 * viscosity / 16.0 + penalty * fields[:, 3 * Z :].reshape(shape))
    cstep[...] = ratio
    for a in range(3):
        force = fields[:, a * Z : (a + 1) * Z].reshape(shape)
        cforce[a] = force
        cvel[0, a, :, mid_rows, :] = ratio * force

    def coarse_div(number, low, count):
        planes, right, left = pl.ds(low, count), pl.ds(low + 1, count), pl.ds(low - 1, count)
        total = cvel[number, 0, right, mid_rows, :] - cvel[number, 0, left, mid_rows, :]
        total = total + (cvel[number, 1, planes, up_rows, :] - cvel[number, 1, planes, down_rows, :])
        along_z = apply(pair_gap, flat(cvel[number, 2, planes, mid_rows, :])).reshape(total.shape)
        return (total + along_z) * (0.125 * pressure_step)

    cpress[pl.ds(1, deep - 2), mid_rows, :] = -coarse_div(0, 1, deep - 2)
    count = deep - 4
    planes, right, left = pl.ds(2, count), pl.ds(3, count), pl.ds(1, count)
    shape = (count, tall, Z)
    slopes = (
        cpress[right, mid_rows, :] - cpress[left, mid_rows, :],
        cpress[planes, up_rows, :] - cpress[planes, down_rows, :],
        apply(pair_gap, flat(cpress[planes, mid_rows, :])).reshape(shape),
    )
    for a in range(3):
        middle = cvel[0, a, planes, mid_rows, :]
        near = cvel[0, a, right, mid_rows, :] + cvel[0, a, left, mid_rows, :]
        near = near + (cvel[0, a, planes, up_rows, :] + cvel[0, a, planes, down_rows, :])
        near = near + apply(pair_sum, flat(middle)).reshape(shape)
        moved = cforce[a, planes] - 0.125 * slopes[a] + (viscosity / 16.0) * near
        cvel[1, a, planes, mid_rows, :] = keep * middle + cstep[planes] * moved
    count = deep - 6
    planes = pl.ds(3, count)
    press = cpress[planes, mid_rows, :] - coarse_div(1, 3, count)
    ends = [cvel[1, a, planes, mid_rows, :] for a in range(3)] + [press]
    for field in range(4):
        cfine[field] = apply(stretch, flat(ends[field])).reshape(count, tall, Z)
    row = lax.broadcasted_iota(jnp.int32, (8, Z), 0)
    lower = row < 2
    upper = row >= 6
    part = ((row + 2) % 4).astype(jnp.float32) * 0.25 + 0.125
    for field in range(4):
        for x in range(count):
            for tile in range((Y + 16) // 8):
                first = cy - 3 + 2 * tile
                lines = [jnp.broadcast_to(cfine[field, x, pl.ds(first + k, 1), :], (8, Z)) for k in range(4)]
                near = jnp.where(lower, lines[0], jnp.where(upper, lines[2], lines[1]))
                far = jnp.where(lower, lines[1], jnp.where(upper, lines[3], lines[2]))
                yfine[field, x, pl.ds(8 * tile, 8), :] = near + part * (far - near)


def solve_kernel(sizes, *refs):
    X, Y, Z = sizes
    cx = X // 4
    yfine, down_ref, up_ref, xl_ref, xr_ref, mask, force_ref = refs[:7]
    velo_out, press_out = refs[7:9]
    force, step, state, mid, sems = refs[9:]
    ex, ey, fy = 4, 16, 8
    deep = cx + 10

    copies = []

    def copy(src, dst):
        made = pltpu.make_async_copy(src, dst, sems.at[len(copies)])
        made.start()
        copies.append(made)
        return made

    second = []
    for field in range(3):
        second.append(copy(force_ref.at[field], force.at[field, pl.ds(ex, X), pl.ds(fy, Y), :]))
    for ref, high in ((xl_ref, False), (xr_ref, True)):
        number = 0
        for field, depth in x_depths:
            x = ex + X if high else ex - depth
            target = step.at[pl.ds(x, depth), pl.ds(fy, Y), :] if field == 3 else force.at[field, pl.ds(x, depth), pl.ds(fy, Y), :]
            second.append(copy(ref.at[pl.ds(number, depth)], target))
            number += depth

    wide = Y + 16
    wide_rows = pl.ds(ey - 8, wide)

    def stretch_x(m, carry):
        for field in range(4):
            low, here, high = yfine[field, m], yfine[field, m + 1], yfine[field, m + 2]
            state[field, 4 * m, wide_rows, :] = 0.375 * low + 0.625 * here
            state[field, 4 * m + 1, wide_rows, :] = 0.125 * low + 0.875 * here
            state[field, 4 * m + 2, wide_rows, :] = 0.875 * here + 0.125 * high
            state[field, 4 * m + 3, wide_rows, :] = 0.625 * here + 0.375 * high
        return carry

    lax.fori_loop(0, cx + 2, stretch_x, 0)

    for made in second:
        made.wait()
    for x in range(X):
        step[ex + x, pl.ds(fy, Y), :] = step_of(mask[x])
    for ref, high in ((down_ref, False), (up_ref, True)):
        number = 0
        for field, depth in y_depths:
            for row in range(depth):
                y = fy + Y + row if high else fy - depth + row
                for x in range(X):
                    place = number * X + x
                    line = ref[deep + 2 + place // 8, pl.ds(place % 8, 1), :]
                    if field == 3:
                        step[ex + x, pl.ds(y, 1), :] = line
                    else:
                        force[field, ex + x, pl.ds(y, 1), :] = line
                number += 1
        for side in range(2):
            for row, (field, dx, dy) in enumerate(corner_cells):
                x = ex - dx if side == 0 else ex + X - 1 + dx
                y = fy + Y - 1 + dy if high else fy - dy
                line = ref[deep + side, pl.ds(row, 1), :]
                if field == 3:
                    step[x, pl.ds(y, 1), :] = line
                else:
                    force[field, x, pl.ds(y, 1), :] = line

    pair_sum, pair_gap = neighbour_matrices(Z, 1)

    def move(old, new, x, count, components, start, size):
        rows, above, below = pl.ds(ey + start, size), pl.ds(ey + start + 1, size), pl.ds(ey + start - 1, size)
        source_rows = pl.ds(fy + start, size)
        planes, right, left = pl.ds(x, count), pl.ds(x + 1, count), pl.ds(x - 1, count)
        shape = (count, size, Z)
        ratio = step[planes, source_rows, :]
        middles = [old[a, planes, rows, :] for a in components]
        sums = apply(pair_sum, jnp.concatenate([flat(v) for v in middles], 0))
        for number, a in enumerate(components):
            if a == 0:
                slope = state[3, right, rows, :] - state[3, left, rows, :]
            elif a == 1:
                slope = state[3, planes, above, :] - state[3, planes, below, :]
            elif 0:
                slope = apply(pair_gap, flat(state[3, planes, rows, :])).reshape(shape)
            else:
                press = state[3, planes, rows, :]
                slope = roll(press, -1) - roll(press, 1)
            near = old[a, right, rows, :] + old[a, left, rows, :]
            near = near + (old[a, planes, above, :] + old[a, planes, below, :])
            near = near + sums[number * count * size : (number + 1) * count * size].reshape(shape)
            source = force[a, planes, source_rows, :]
            if a == 0:
                source = source + mean_drive
            source = source - 0.5 * slope + near
            new[a, planes, rows, :] = keep * middles[number] + ratio * source

    def divergence(vel, x, count, start, size):
        rows, above, below = pl.ds(ey + start, size), pl.ds(ey + start + 1, size), pl.ds(ey + start - 1, size)
        planes, right, left = pl.ds(x, count), pl.ds(x + 1, count), pl.ds(x - 1, count)
        total = (vel[0, right, rows, :] - vel[0, left, rows, :]) + (vel[1, planes, above, :] - vel[1, planes, below, :])
        along_z = vel[2, planes, rows, :]
        if 1:
            total = total + apply(pair_gap, flat(along_z)).reshape(total.shape)
        else:
            total = total + (roll(along_z, -1) - roll(along_z, 1))
        return total * (0.5 * pressure_step)

    def loop(low, high, most, body):
        count = max(n for n in range(1, most + 1) if (high - low) % n == 0)

        def run(number, carry):
            body(low + number * count, count)
            return carry

        lax.fori_loop(0, (high - low) // count, run, 0)

    loop(1, X + 7, 30, lambda x, count: move(state, mid, x, count, (0, 1, 2), -8, wide))

    def press_first(x, count):
        planes = pl.ds(x, count)
        state[3, planes, wide_rows, :] = state[3, planes, wide_rows, :] - divergence(mid, x, count, -8, wide)

    loop(2, X + 6, 28, press_first)
    move(mid, state, ex - 1, 1, (0,), 0, Y)
    move(mid, state, ex + X, 1, (0,), 0, Y)

    def second_move(x, count):
        move(mid, state, x, count, (0, 2), 0, Y)
        move(mid, state, x, count, (1,), -8, wide)

    loop(ex, ex + X, 24, second_move)
    inner = pl.ds(ey, Y)
    last = [copy(state.at[a, pl.ds(ex, X), inner, :], velo_out.at[a]) for a in range(3)]

    def press_second(x, count):
        planes = pl.ds(x, count)
        step[planes, pl.ds(fy, Y), :] = state[3, planes, inner, :] - divergence(state, x, count, 0, Y)

    loop(ex, ex + X, 24, press_second)
    last.append(copy(step.at[pl.ds(ex, X), pl.ds(fy, Y), :], press_out))
    for made in last:
        made.wait()


def relay_kernel(sizes, ml_ref, mp_ref, mr_ref, yp_ref, ym_ref, up_ref, down_ref):
    cx = sizes[0] // 4
    for ref, lines, corner in ((down_ref, yp_ref, cx), (up_ref, ym_ref, cx + 1)):
        ref[pl.ds(0, 5)] = ml_ref[pl.ds(cx - 5, 5)]
        ref[pl.ds(5, cx)] = mp_ref[pl.ds(0, cx)]
        ref[pl.ds(5 + cx, 5)] = mr_ref[pl.ds(0, 5)]
        ref[cx + 10] = ml_ref[corner]
        ref[cx + 11] = mr_ref[corner]
        ref[pl.ds(cx + 12, lines.shape[0])] = lines[...]


def shift(value, axis, by):
    count = lax.axis_size(axis)
    return lax.ppermute(value, axis, [(i, (i + by) % count) for i in range(count)])


def shards(solid_mask, forcing):
    X, Y, Z = sizes = solid_mask.shape
    cx, cy = X // 4, Y // 4
    f32 = jnp.float32
    made = jax.ShapeDtypeStruct
    vmem = pltpu.VMEM
    anywhere = pl.BlockSpec(memory_space=pl.ANY)
    near = pl.BlockSpec(memory_space=vmem)
    message = made((cx + 2, 8, Z), f32)
    planes = made((10, Y, Z), f32)
    lines = made((10 * X // 8, 8, Z), f32)
    mp, mm, xp, xm, yp, ym, mask, force = pl.pallas_call(
        functools.partial(pack_kernel, sizes),
        out_shape=(message, message, planes, planes, lines, lines, made((X * Y, Z), jnp.int32), made((3 * X * Y, Z), f32)),
        in_specs=[pl.BlockSpec(memory_space=pltpu.HBM)] * 2,
        out_specs=[near] * 8,
        scratch_shapes=[vmem((4, cx, Y, Z), f32), pltpu.SemaphoreType.DMA((4,))],
        compiler_params=pltpu.CompilerParams(vmem_limit_bytes=12 * 2**20),
        name="pack",
    )(
        pltpu.with_memory_space_constraint(solid_mask.reshape(X * Y, Z), pltpu.HBM),
        pltpu.with_memory_space_constraint(forcing.reshape(3 * X * Y, Z), pltpu.HBM),
    )
    xl = shift(xp, "grp", 1)
    xr = shift(xm, "grp", -1)
    ml = shift(mp, "grp", 1)
    mr = shift(mm, "grp", -1)
    joined = made((cx + 12 + 10 * X // 8, 8, Z), f32)
    to_up, to_down = pl.pallas_call(
        functools.partial(relay_kernel, sizes),
        out_shape=(joined, joined),
        in_specs=[near] * 5,
        out_specs=[near] * 2,
        compiler_params=pltpu.CompilerParams(vmem_limit_bytes=2 * 2**20),
        name="relay",
    )(ml, mp, mr, yp, ym)
    down = shift(to_down, "dev", 1)
    up = shift(to_up, "dev", -1)
    tall, deep = 3 * cy, cx + 10
    yfine = pl.pallas_call(
        functools.partial(coarse_kernel, sizes),
        out_shape=made((4, cx + 4, Y + 16, Z), f32),
        in_specs=[near] * 5,
        out_specs=near,
        scratch_shapes=[
            vmem((3, deep, tall, Z), f32),
            vmem((deep, tall, Z), f32),
            vmem((2, 3, deep, tall + 2 * cy, Z), f32),
            vmem((deep, tall + 2 * cy, Z), f32),
            vmem((4, cx + 4, tall, Z), f32),
        ],
        compiler_params=pltpu.CompilerParams(vmem_limit_bytes=16 * 2**20),
        name="coarse",
    )(down, up, ml, mp, mr)
    return pl.pallas_call(
        functools.partial(solve_kernel, sizes),
        out_shape=(made((3, X, Y, Z), f32), made((X, Y, Z), f32)),
        in_specs=[near] * 7,
        out_specs=(anywhere, anywhere),
        scratch_shapes=[
            vmem((3, X + 8, Y + 16, Z), f32),
            vmem((X + 8, Y + 16, Z), f32),
            vmem((4, X + 8, Y + 32, Z), f32),
            vmem((3, X + 8, Y + 32, Z), f32),
            pltpu.SemaphoreType.DMA((20,)),
        ],
        compiler_params=pltpu.CompilerParams(vmem_limit_bytes=32 * 2**20),
        name="solve",
    )(yfine, down, up, xl, xr, mask.reshape(X, Y, Z), force.reshape(3, X, Y, Z))


def solution(mesh):
    in_specs = (P("grp", "dev", None), P(None, "grp", "dev", None))
    out_specs = (P(None, "grp", "dev", None), P("grp", "dev", None))
    return jax.shard_map(shards, mesh=mesh, in_specs=in_specs, out_specs=out_specs, check_vma=False)
```

```python
import functools

import jax
import jax.numpy as jnp
from jax import lax
from jax.experimental import pallas as pl
from jax.experimental.pallas import tpu as pltpu
from jax.sharding import PartitionSpec as P

viscosity = 1.0
penalty = 10.0
relaxation = 0.8
pressure_step = 1.0
mean_drive = 1.0

keep = 1.0 - relaxation
pore_step = relaxation / (6.0 * viscosity)
solid_step = relaxation / (6.0 * viscosity + penalty)

x_depths = ((0, 3), (1, 2), (2, 2), (3, 3))
y_depths = ((0, 2), (1, 3), (2, 2), (3, 3))
corner_cells = ((0, 1, 1), (0, 1, 2), (1, 1, 1), (1, 2, 1), (3, 1, 1), (3, 1, 2), (3, 2, 1))


def roll(value, shift):
    return pltpu.roll(value, shift % value.shape[-1], value.ndim - 1)


def lane_phase(shape):
    return lax.broadcasted_iota(jnp.int32, shape, len(shape) - 1) % 4


def neighbour_matrices(Z, distance):
    source = lax.broadcasted_iota(jnp.int32, (2 * Z, Z), 0) % Z
    target = lax.broadcasted_iota(jnp.int32, (2 * Z, Z), 1)
    after = (source == (target + distance) % Z).astype(jnp.float32)
    before = (source == (target + Z - distance) % Z).astype(jnp.float32)
    return (after + before).astype(jnp.bfloat16), (after - before).astype(jnp.bfloat16)


def apply(matrix, values):
    high = values.astype(jnp.bfloat16)
    low = (values - high.astype(jnp.float32)).astype(jnp.bfloat16)
    return jnp.dot(jnp.concatenate([high, low], -1), matrix, preferred_element_type=jnp.float32)


def flat(values):
    return values.reshape(-1, values.shape[-1])


def step_of(mask):
    return jnp.where(mask != 0, solid_step, pore_step).astype(jnp.float32)


def pack_kernel(sizes, mask_in, force_in, mp_ref, mm_ref, xp_ref, xm_ref, mask_ref, force_ref, sums, sems):
    X, Y, Z = sizes
    cx, cy = X // 4, Y // 4
    copies = [
        pltpu.make_async_copy(mask_in, mask_ref, sems.at[3]),
    ]
    for field in range(3):
        part = pl.ds(field * X * Y, X * Y)
        copies.append(pltpu.make_async_copy(force_in.at[part], force_ref.at[part], sems.at[field]))
    for made in copies:
        made.start()
    for made in copies:
        made.wait()

    def rows(field, index):
        if field == 3:
            return mask_ref[index, :]
        base = field * X * Y
        moved = pl.ds(base + index.start, index.size, index.stride)
        return force_ref[moved, :]

    def values(field, start, size, stride=1):
        taken = rows(field, pl.ds(start, size, stride))
        return step_of(taken) if field == 3 else taken

    phase = lane_phase((cy, Z))
    means = []
    for field in range(4):
        for block in range(cx):
            total = None
            for plane in range(4):
                part = rows(field, pl.ds((4 * block + plane) * Y, Y)).astype(jnp.float32)
                total = part if total is None else total + part
            sums[field, block] = total
    for block in range(cx):
        packed = None
        for field in range(4):
            total = sums[field, block, pl.ds(0, cy, 4), :]
            for row in range(1, 4):
                total = total + sums[field, block, pl.ds(row, cy, 4), :]
            total = total + jnp.where(phase % 2 == 0, roll(total, -1), roll(total, 1))
            total = total + jnp.where(phase < 2, roll(total, -2), roll(total, 2))
            mean = total * (1.0 / 64.0)
            if field == 0:
                mean = mean + mean_drive
            packed = mean if packed is None else jnp.where(phase == field, mean, packed)
        mp_ref[block] = packed
        mm_ref[block] = packed
    for ref, top in ((mp_ref, True), (mm_ref, False)):
        for high in (True, False):
            for number, (field, dx, dy) in enumerate(corner_cells):
                x = X - dx if high else dx - 1
                y = Y - dy if top else dy - 1
                ref[cx + (0 if high else 1), pl.ds(number, 1), :] = values(field, x * Y + y, 1)
            ref[cx + (0 if high else 1), pl.ds(7, 1), :] = jnp.zeros((1, Z), jnp.float32)
    for ref, high in ((xp_ref, True), (xm_ref, False)):
        number = 0
        for field, depth in x_depths:
            for plane in range(depth):
                x = X - depth + plane if high else plane
                ref[number] = values(field, x * Y, Y)
                number += 1
    for ref, high in ((mp_ref, True), (mm_ref, False)):
        number = 0
        for field, depth in y_depths:
            for row in range(depth):
                y = Y - depth + row if high else row
                line = values(field, y, X, Y)
                for tile in range(X // 8):
                    ref[cx + 2 + number * (X // 8) + tile] = line[8 * tile : 8 * tile + 8]
                number += 1


def coarse_kernel(sizes, left_ref, right_ref, md_ref, mp_ref, mu_ref, yfine, cforce, cstep, cvel, cpress, cfine):
    X, Y, Z = sizes
    cx, cy = X // 4, Y // 4
    tall, deep = 3 * cy, cx + 10
    mid_rows, up_rows, down_rows = pl.ds(cy, tall), pl.ds(cy + 1, tall), pl.ds(cy - 1, tall)
    source = lax.broadcasted_iota(jnp.int32, (2 * Z, 4 * Z), 0) % Z
    target = lax.broadcasted_iota(jnp.int32, (2 * Z, 4 * Z), 1)
    spread = (source == (target % Z) // 4 * 4 + target // Z).astype(jnp.float32).astype(jnp.bfloat16)
    pair_sum, pair_gap = neighbour_matrices(Z, 4)
    source = lax.broadcasted_iota(jnp.int32, (2 * Z, Z), 0) % Z
    target = lax.broadcasted_iota(jnp.int32, (2 * Z, Z), 1)
    part = ((target + 2) % 4).astype(jnp.float32) * 0.25 + 0.125
    stretch = jnp.where(source == (target + Z - 2) % Z, 1.0 - part, 0.0) + jnp.where(source == (target + 2) % Z, part, 0.0)
    stretch = stretch.astype(jnp.bfloat16)

    packed = []
    for x in range(deep):
        if 5 <= x < cx + 5:
            packed += [md_ref[x - 5], mp_ref[x - 5], mu_ref[x - 5]]
        else:
            side, plane = (left_ref, x) if x < 5 else (right_ref, x - 5 - cx)
            packed += [side[plane], side[5 + plane], side[10 + plane]]
    fields = apply(spread, jnp.concatenate(packed, 0))
    shape = (deep, tall, Z)
    ratio = relaxation / (6.0 * viscosity / 16.0 + penalty * fields[:, 3 * Z :].reshape(shape))
    cstep[...] = ratio
    for a in range(3):
        force = fields[:, a * Z : (a + 1) * Z].reshape(shape)
        cforce[a] = force
        cvel[0, a, :, mid_rows, :] = ratio * force

    def coarse_div(number, low, count):
        planes, right, left = pl.ds(low, count), pl.ds(low + 1, count), pl.ds(low - 1, count)
        total = cvel[number, 0, right, mid_rows, :] - cvel[number, 0, left, mid_rows, :]
        total = total + (cvel[number, 1, planes, up_rows, :] - cvel[number, 1, planes, down_rows, :])
        along_z = apply(pair_gap, flat(cvel[number, 2, planes, mid_rows, :])).reshape(total.shape)
        return (total + along_z) * (0.125 * pressure_step)

    cpress[pl.ds(1, deep - 2), mid_rows, :] = -coarse_div(0, 1, deep - 2)
    count = deep - 4
    planes, right, left = pl.ds(2, count), pl.ds(3, count), pl.ds(1, count)
    shape = (count, tall, Z)
    slopes = (
        cpress[right, mid_rows, :] - cpress[left, mid_rows, :],
        cpress[planes, up_rows, :] - cpress[planes, down_rows, :],
        apply(pair_gap, flat(cpress[planes, mid_rows, :])).reshape(shape),
    )
    for a in range(3):
        middle = cvel[0, a, planes, mid_rows, :]
        near = cvel[0, a, right, mid_rows, :] + cvel[0, a, left, mid_rows, :]
        near = near + (cvel[0, a, planes, up_rows, :] + cvel[0, a, planes, down_rows, :])
        near = near + apply(pair_sum, flat(middle)).reshape(shape)
        moved = cforce[a, planes] - 0.125 * slopes[a] + (viscosity / 16.0) * near
        cvel[1, a, planes, mid_rows, :] = keep * middle + cstep[planes] * moved
    count = deep - 6
    planes = pl.ds(3, count)
    press = cpress[planes, mid_rows, :] - coarse_div(1, 3, count)
    ends = [cvel[1, a, planes, mid_rows, :] for a in range(3)] + [press]
    for field in range(4):
        cfine[field] = apply(stretch, flat(ends[field])).reshape(count, tall, Z)
    row = lax.broadcasted_iota(jnp.int32, (8, Z), 0)
    lower = row < 2
    upper = row >= 6
    part = ((row + 2) % 4).astype(jnp.float32) * 0.25 + 0.125
    for field in range(4):
        for x in range(count):
            for tile in range((Y + 16) // 8):
                first = cy - 3 + 2 * tile
                lines = [jnp.broadcast_to(cfine[field, x, pl.ds(first + k, 1), :], (8, Z)) for k in range(4)]
                near = jnp.where(lower, lines[0], jnp.where(upper, lines[2], lines[1]))
                far = jnp.where(lower, lines[1], jnp.where(upper, lines[3], lines[2]))
                yfine[field, x, pl.ds(8 * tile, 8), :] = near + part * (far - near)


def solve_kernel(sizes, *refs):
    X, Y, Z = sizes
    cx = X // 4
    yfine, left_ref, right_ref, yd_ref, yu_ref, xl_ref, xr_ref, mask, force_ref = refs[:9]
    velo_out, press_out = refs[9:11]
    force, step, state, mid, sems = refs[11:]
    ex, ey, fy = 4, 16, 8
    deep = cx + 10

    copies = []

    def copy(src, dst):
        made = pltpu.make_async_copy(src, dst, sems.at[len(copies)])
        made.start()
        copies.append(made)
        return made

    second = []
    for field in range(3):
        second.append(copy(force_ref.at[field], force.at[field, pl.ds(ex, X), pl.ds(fy, Y), :]))
    for ref, high in ((xl_ref, False), (xr_ref, True)):
        number = 0
        for field, depth in x_depths:
            x = ex + X if high else ex - depth
            target = step.at[pl.ds(x, depth), pl.ds(fy, Y), :] if field == 3 else force.at[field, pl.ds(x, depth), pl.ds(fy, Y), :]
            second.append(copy(ref.at[pl.ds(number, depth)], target))
            number += depth

    wide = Y + 16
    wide_rows = pl.ds(ey - 8, wide)

    def stretch_x(m, carry):
        for field in range(4):
            low, here, high = yfine[field, m], yfine[field, m + 1], yfine[field, m + 2]
            state[field, 4 * m, wide_rows, :] = 0.375 * low + 0.625 * here
            state[field, 4 * m + 1, wide_rows, :] = 0.125 * low + 0.875 * here
            state[field, 4 * m + 2, wide_rows, :] = 0.875 * here + 0.125 * high
            state[field, 4 * m + 3, wide_rows, :] = 0.625 * here + 0.375 * high
        return carry

    lax.fori_loop(0, cx + 2, stretch_x, 0)

    for made in second:
        made.wait()
    for x in range(X):
        step[ex + x, pl.ds(fy, Y), :] = step_of(mask[x])
    for ref, high in ((yd_ref, False), (yu_ref, True)):
        number = 0
        for field, depth in y_depths:
            for row in range(depth):
                y = fy + Y + row if high else fy - depth + row
                for x in range(X):
                    place = number * X + x
                    line = ref[cx + 2 + place // 8, pl.ds(place % 8, 1), :]
                    if field == 3:
                        step[ex + x, pl.ds(y, 1), :] = line
                    else:
                        force[field, ex + x, pl.ds(y, 1), :] = line
                number += 1
        for side, corner_ref in enumerate((left_ref, right_ref)):
            for row, (field, dx, dy) in enumerate(corner_cells):
                x = ex - dx if side == 0 else ex + X - 1 + dx
                y = fy + Y - 1 + dy if high else fy - dy
                line = corner_ref[16 if high else 15, pl.ds(row, 1), :]
                if field == 3:
                    step[x, pl.ds(y, 1), :] = line
                else:
                    force[field, x, pl.ds(y, 1), :] = line

    pair_sum, pair_gap = neighbour_matrices(Z, 1)

    def move(old, new, x, count, components, start, size):
        rows, above, below = pl.ds(ey + start, size), pl.ds(ey + start + 1, size), pl.ds(ey + start - 1, size)
        source_rows = pl.ds(fy + start, size)
        planes, right, left = pl.ds(x, count), pl.ds(x + 1, count), pl.ds(x - 1, count)
        shape = (count, size, Z)
        ratio = step[planes, source_rows, :]
        middles = [old[a, planes, rows, :] for a in components]
        sums = apply(pair_sum, jnp.concatenate([flat(v) for v in middles], 0))
        for number, a in enumerate(components):
            if a == 0:
                slope = state[3, right, rows, :] - state[3, left, rows, :]
            elif a == 1:
                slope = state[3, planes, above, :] - state[3, planes, below, :]
            elif 0:
                slope = apply(pair_gap, flat(state[3, planes, rows, :])).reshape(shape)
            else:
                press = state[3, planes, rows, :]
                slope = roll(press, -1) - roll(press, 1)
            near = old[a, right, rows, :] + old[a, left, rows, :]
            near = near + (old[a, planes, above, :] + old[a, planes, below, :])
            near = near + sums[number * count * size : (number + 1) * count * size].reshape(shape)
            source = force[a, planes, source_rows, :]
            if a == 0:
                source = source + mean_drive
            source = source - 0.5 * slope + near
            new[a, planes, rows, :] = keep * middles[number] + ratio * source

    def divergence(vel, x, count, start, size):
        rows, above, below = pl.ds(ey + start, size), pl.ds(ey + start + 1, size), pl.ds(ey + start - 1, size)
        planes, right, left = pl.ds(x, count), pl.ds(x + 1, count), pl.ds(x - 1, count)
        total = (vel[0, right, rows, :] - vel[0, left, rows, :]) + (vel[1, planes, above, :] - vel[1, planes, below, :])
        along_z = vel[2, planes, rows, :]
        if 1:
            total = total + apply(pair_gap, flat(along_z)).reshape(total.shape)
        else:
            total = total + (roll(along_z, -1) - roll(along_z, 1))
        return total * (0.5 * pressure_step)

    def loop(low, high, most, body):
        count = max(n for n in range(1, most + 1) if (high - low) % n == 0)

        def run(number, carry):
            body(low + number * count, count)
            return carry

        lax.fori_loop(0, (high - low) // count, run, 0)

    loop(1, X + 7, 30, lambda x, count: move(state, mid, x, count, (0, 1, 2), -8, wide))

    def press_first(x, count):
        planes = pl.ds(x, count)
        state[3, planes, wide_rows, :] = state[3, planes, wide_rows, :] - divergence(mid, x, count, -8, wide)

    loop(2, X + 6, 28, press_first)
    move(mid, state, ex - 1, 1, (0,), 0, Y)
    move(mid, state, ex + X, 1, (0,), 0, Y)

    def second_move(x, count):
        move(mid, state, x, count, (0, 2), 0, Y)
        move(mid, state, x, count, (1,), -8, wide)

    loop(ex, ex + X, 24, second_move)
    inner = pl.ds(ey, Y)
    last = [copy(state.at[a, pl.ds(ex, X), inner, :], velo_out.at[a]) for a in range(3)]

    def press_second(x, count):
        planes = pl.ds(x, count)
        step[planes, pl.ds(fy, Y), :] = state[3, planes, inner, :] - divergence(state, x, count, 0, Y)

    loop(ex, ex + X, 24, press_second)
    last.append(copy(step.at[pl.ds(ex, X), pl.ds(fy, Y), :], press_out))
    for made in last:
        made.wait()


def relay_kernel(sizes, mu_ref, mp_ref, md_ref, right_ref, left_ref):
    cx = sizes[0] // 4
    for ref, start, corner in ((right_ref, cx - 5, cx), (left_ref, 0, cx + 1)):
        for number, source in enumerate((md_ref, mp_ref, mu_ref)):
            ref[pl.ds(5 * number, 5)] = source[pl.ds(start, 5)]
        ref[15] = md_ref[corner]
        ref[16] = mu_ref[corner]


def shift(value, axis, by):
    count = lax.axis_size(axis)
    return lax.ppermute(value, axis, [(i, (i + by) % count) for i in range(count)])


def shards(solid_mask, forcing):
    X, Y, Z = sizes = solid_mask.shape
    cx, cy = X // 4, Y // 4
    f32 = jnp.float32
    made = jax.ShapeDtypeStruct
    vmem = pltpu.VMEM
    anywhere = pl.BlockSpec(memory_space=pl.ANY)
    near = pl.BlockSpec(memory_space=vmem)
    message = made((cx + 2 + 10 * X // 8, 8, Z), f32)
    planes = made((10, Y, Z), f32)
    mp, mm, xp, xm, mask, force = pl.pallas_call(
        functools.partial(pack_kernel, sizes),
        out_shape=(message, message, planes, planes, made((X * Y, Z), jnp.int32), made((3 * X * Y, Z), f32)),
        in_specs=[pl.BlockSpec(memory_space=pltpu.HBM)] * 2,
        out_specs=[near] * 6,
        scratch_shapes=[vmem((4, cx, Y, Z), f32), pltpu.SemaphoreType.DMA((4,))],
        compiler_params=pltpu.CompilerParams(vmem_limit_bytes=12 * 2**20),
        name="pack",
    )(
        pltpu.with_memory_space_constraint(solid_mask.reshape(X * Y, Z), pltpu.HBM),
        pltpu.with_memory_space_constraint(forcing.reshape(3 * X * Y, Z), pltpu.HBM),
    )
    md = shift(mp, "dev", 1)
    mu = shift(mm, "dev", -1)
    xl = shift(xp, "grp", 1)
    xr = shift(xm, "grp", -1)
    joined = made((17, 8, Z), f32)
    to_right, to_left = pl.pallas_call(
        functools.partial(relay_kernel, sizes),
        out_shape=(joined, joined),
        in_specs=[near] * 3,
        out_specs=[near] * 2,
        compiler_params=pltpu.CompilerParams(vmem_limit_bytes=2 * 2**20),
        name="relay",
    )(mu, mm, md)
    left = shift(to_right, "grp", 1)
    right = shift(to_left, "grp", -1)
    tall, deep = 3 * cy, cx + 10
    yfine = pl.pallas_call(
        functools.partial(coarse_kernel, sizes),
        out_shape=made((4, cx + 4, Y + 16, Z), f32),
        in_specs=[near] * 5,
        out_specs=near,
        scratch_shapes=[
            vmem((3, deep, tall, Z), f32),
            vmem((deep, tall, Z), f32),
            vmem((2, 3, deep, tall + 2 * cy, Z), f32),
            vmem((deep, tall + 2 * cy, Z), f32),
            vmem((4, cx + 4, tall, Z), f32),
        ],
        compiler_params=pltpu.CompilerParams(vmem_limit_bytes=16 * 2**20),
        name="coarse",
    )(left, right, md, mm, mu)
    return pl.pallas_call(
        functools.partial(solve_kernel, sizes),
        out_shape=(made((3, X, Y, Z), f32), made((X, Y, Z), f32)),
        in_specs=[near] * 9,
        out_specs=(anywhere, anywhere),
        scratch_shapes=[
            vmem((3, X + 8, Y + 16, Z), f32),
            vmem((X + 8, Y + 16, Z), f32),
            vmem((4, X + 8, Y + 32, Z), f32),
            vmem((3, X + 8, Y + 32, Z), f32),
            pltpu.SemaphoreType.DMA((20,)),
        ],
        compiler_params=pltpu.CompilerParams(vmem_limit_bytes=32 * 2**20),
        name="solve",
    )(yfine, left, right, md, mu, xl, xr, mask.reshape(X, Y, Z), force.reshape(3, X, Y, Z))


def solution(mesh):
    in_specs = (P("grp", "dev", None), P(None, "grp", "dev", None))
    out_specs = (P(None, "grp", "dev", None), P("grp", "dev", None))
    return jax.shard_map(shards, mesh=mesh, in_specs=in_specs, out_specs=out_specs, check_vma=False)
```

```python
import functools

import jax
import jax.numpy as jnp
from jax import lax
from jax.experimental import pallas as pl
from jax.experimental.pallas import tpu as pltpu
from jax.sharding import PartitionSpec as P

viscosity = 1.0
penalty = 10.0
relaxation = 0.8
pressure_step = 1.0
mean_drive = 1.0

keep = 1.0 - relaxation
pore_step = relaxation / (6.0 * viscosity)
solid_step = relaxation / (6.0 * viscosity + penalty)

x_depths = ((0, 3), (1, 2), (2, 2), (3, 3))
y_depths = ((0, 2), (1, 3), (2, 2), (3, 3))
corner_cells = ((0, 1, 1), (0, 1, 2), (1, 1, 1), (1, 2, 1), (3, 1, 1), (3, 1, 2), (3, 2, 1))


def roll(value, shift):
    return pltpu.roll(value, shift % value.shape[-1], value.ndim - 1)


def lane_phase(shape):
    return lax.broadcasted_iota(jnp.int32, shape, len(shape) - 1) % 4


def neighbour_matrices(Z, distance):
    source = lax.broadcasted_iota(jnp.int32, (2 * Z, Z), 0) % Z
    target = lax.broadcasted_iota(jnp.int32, (2 * Z, Z), 1)
    after = (source == (target + distance) % Z).astype(jnp.float32)
    before = (source == (target + Z - distance) % Z).astype(jnp.float32)
    return (after + before).astype(jnp.bfloat16), (after - before).astype(jnp.bfloat16)


def apply(matrix, values):
    high = values.astype(jnp.bfloat16)
    low = (values - high.astype(jnp.float32)).astype(jnp.bfloat16)
    return jnp.dot(jnp.concatenate([high, low], -1), matrix, preferred_element_type=jnp.float32)


def flat(values):
    return values.reshape(-1, values.shape[-1])


def step_of(mask):
    return jnp.where(mask != 0, solid_step, pore_step).astype(jnp.float32)


def pack_kernel(sizes, mask_in, force_in, own_ref, mp_ref, mm_ref, xp_ref, xm_ref, mask_ref, force_ref, sums, sems):
    X, Y, Z = sizes
    cx, cy = X // 4, Y // 4
    copies = [
        pltpu.make_async_copy(mask_in, mask_ref, sems.at[3]),
    ]
    for field in range(3):
        part = pl.ds(field * X * Y, X * Y)
        copies.append(pltpu.make_async_copy(force_in.at[part], force_ref.at[part], sems.at[field]))
    for made in copies:
        made.start()
    for made in copies:
        made.wait()

    def rows(field, index):
        if field == 3:
            return mask_ref[index, :]
        base = field * X * Y
        moved = pl.ds(base + index.start, index.size, index.stride)
        return force_ref[moved, :]

    def values(field, start, size, stride=1):
        taken = rows(field, pl.ds(start, size, stride))
        return step_of(taken) if field == 3 else taken

    phase = lane_phase((cy, Z))
    means = []
    for field in range(4):
        for block in range(cx):
            total = None
            for plane in range(4):
                part = rows(field, pl.ds((4 * block + plane) * Y, Y)).astype(jnp.float32)
                total = part if total is None else total + part
            sums[field, block] = total
    for block in range(cx):
        packed = None
        for field in range(4):
            total = sums[field, block, pl.ds(0, cy, 4), :]
            for row in range(1, 4):
                total = total + sums[field, block, pl.ds(row, cy, 4), :]
            total = total + jnp.where(phase % 2 == 0, roll(total, -1), roll(total, 1))
            total = total + jnp.where(phase < 2, roll(total, -2), roll(total, 2))
            mean = total * (1.0 / 64.0)
            if field == 0:
                mean = mean + mean_drive
            packed = mean if packed is None else jnp.where(phase == field, mean, packed)
        own_ref[block] = packed
        mp_ref.reshape(-1, Z)[pl.ds(5 * block, 5), :] = packed[cy - 5 :]
        mm_ref.reshape(-1, Z)[pl.ds(5 * block, 5), :] = packed[:5]
    own_tiles = -(-5 * cx // 8)
    for ref in (mp_ref, mm_ref):
        ref.reshape(-1, Z)[pl.ds(5 * cx, 8 * own_tiles - 5 * cx), :] = jnp.zeros((8 * own_tiles - 5 * cx, Z), jnp.float32)
    for ref, top in ((mp_ref, True), (mm_ref, False)):
        for high in (True, False):
            for number, (field, dx, dy) in enumerate(corner_cells):
                x = X - dx if high else dx - 1
                y = Y - dy if top else dy - 1
                ref[own_tiles + (0 if high else 1), pl.ds(number, 1), :] = values(field, x * Y + y, 1)
            ref[own_tiles + (0 if high else 1), pl.ds(7, 1), :] = jnp.zeros((1, Z), jnp.float32)
    for ref, high in ((xp_ref, True), (xm_ref, False)):
        number = 0
        for field, depth in x_depths:
            for plane in range(depth):
                x = X - depth + plane if high else plane
                ref[number] = values(field, x * Y, Y)
                number += 1
    for ref, high in ((mp_ref, True), (mm_ref, False)):
        number = 0
        for field, depth in y_depths:
            for row in range(depth):
                y = Y - depth + row if high else row
                line = values(field, y, X, Y)
                for tile in range(X // 8):
                    ref[own_tiles + 2 + number * (X // 8) + tile] = line[8 * tile : 8 * tile + 8]
                number += 1


def coarse_kernel(sizes, left_ref, right_ref, md_ref, own_ref, low_ref, mu_ref, yfine, gathered, cforce, cstep, cvel, cpress, cfine):
    X, Y, Z = sizes
    cx, cy = X // 4, Y // 4
    tall, deep = 3 * cy, cx + 10
    mid_rows, up_rows, down_rows = pl.ds(cy, tall), pl.ds(cy + 1, tall), pl.ds(cy - 1, tall)
    source = lax.broadcasted_iota(jnp.int32, (2 * Z, 4 * Z), 0) % Z
    target = lax.broadcasted_iota(jnp.int32, (2 * Z, 4 * Z), 1)
    spread = (source == (target % Z) // 4 * 4 + target // Z).astype(jnp.float32).astype(jnp.bfloat16)
    pair_sum, pair_gap = neighbour_matrices(Z, 4)
    source = lax.broadcasted_iota(jnp.int32, (2 * Z, Z), 0) % Z
    target = lax.broadcasted_iota(jnp.int32, (2 * Z, Z), 1)
    part = ((target + 2) % 4).astype(jnp.float32) * 0.25 + 0.125
    stretch = jnp.where(source == (target + Z - 2) % Z, 1.0 - part, 0.0) + jnp.where(source == (target + 2) % Z, part, 0.0)
    stretch = stretch.astype(jnp.bfloat16)

    far = jnp.zeros((deep, cy - 5, Z), jnp.float32)
    gathered[:, pl.ds(0, cy - 5), :] = far
    gathered[:, pl.ds(2 * cy + 5, cy - 5), :] = far
    below, above = pl.ds(cy - 5, 5), pl.ds(2 * cy, 5)
    for x in range(deep):
        if 5 <= x < cx + 5:
            rows = pl.ds(5 * (x - 5), 5)
            gathered[x, below, :] = md_ref.reshape(-1, Z)[rows, :]
            gathered[x, pl.ds(cy, 5), :] = low_ref.reshape(-1, Z)[rows, :]
            gathered[x, pl.ds(cy + 5, cy - 5), :] = own_ref[x - 5, pl.ds(5, cy - 5), :]
            gathered[x, above, :] = mu_ref.reshape(-1, Z)[rows, :]
        else:
            side, plane = (left_ref, x) if x < 5 else (right_ref, x - 5 - cx)
            gathered[x, below, :] = side[plane, below, :]
            gathered[x, pl.ds(cy, cy), :] = side[5 + plane]
            gathered[x, above, :] = side[10 + plane, pl.ds(0, 5), :]
    fields = apply(spread, flat(gathered[...]))
    shape = (deep, tall, Z)
    ratio = relaxation / (6.0 * viscosity / 16.0 + penalty * fields[:, 3 * Z :].reshape(shape))
    cstep[...] = ratio
    for a in range(3):
        force = fields[:, a * Z : (a + 1) * Z].reshape(shape)
        cforce[a] = force
        cvel[0, a, :, mid_rows, :] = ratio * force

    def coarse_div(number, low, count):
        planes, right, left = pl.ds(low, count), pl.ds(low + 1, count), pl.ds(low - 1, count)
        total = cvel[number, 0, right, mid_rows, :] - cvel[number, 0, left, mid_rows, :]
        total = total + (cvel[number, 1, planes, up_rows, :] - cvel[number, 1, planes, down_rows, :])
        along_z = apply(pair_gap, flat(cvel[number, 2, planes, mid_rows, :])).reshape(total.shape)
        return (total + along_z) * (0.125 * pressure_step)

    cpress[pl.ds(1, deep - 2), mid_rows, :] = -coarse_div(0, 1, deep - 2)
    count = deep - 4
    planes, right, left = pl.ds(2, count), pl.ds(3, count), pl.ds(1, count)
    shape = (count, tall, Z)
    slopes = (
        cpress[right, mid_rows, :] - cpress[left, mid_rows, :],
        cpress[planes, up_rows, :] - cpress[planes, down_rows, :],
        apply(pair_gap, flat(cpress[planes, mid_rows, :])).reshape(shape),
    )
    for a in range(3):
        middle = cvel[0, a, planes, mid_rows, :]
        near = cvel[0, a, right, mid_rows, :] + cvel[0, a, left, mid_rows, :]
        near = near + (cvel[0, a, planes, up_rows, :] + cvel[0, a, planes, down_rows, :])
        near = near + apply(pair_sum, flat(middle)).reshape(shape)
        moved = cforce[a, planes] - 0.125 * slopes[a] + (viscosity / 16.0) * near
        cvel[1, a, planes, mid_rows, :] = keep * middle + cstep[planes] * moved
    count = deep - 6
    planes = pl.ds(3, count)
    press = cpress[planes, mid_rows, :] - coarse_div(1, 3, count)
    ends = [cvel[1, a, planes, mid_rows, :] for a in range(3)] + [press]
    for field in range(4):
        cfine[field] = apply(stretch, flat(ends[field])).reshape(count, tall, Z)
    row = lax.broadcasted_iota(jnp.int32, (8, Z), 0)
    lower = row < 2
    upper = row >= 6
    part = ((row + 2) % 4).astype(jnp.float32) * 0.25 + 0.125
    for field in range(4):
        for x in range(count):
            for tile in range((Y + 16) // 8):
                first = cy - 3 + 2 * tile
                lines = [jnp.broadcast_to(cfine[field, x, pl.ds(first + k, 1), :], (8, Z)) for k in range(4)]
                near = jnp.where(lower, lines[0], jnp.where(upper, lines[2], lines[1]))
                far = jnp.where(lower, lines[1], jnp.where(upper, lines[3], lines[2]))
                yfine[field, x, pl.ds(8 * tile, 8), :] = near + part * (far - near)


def solve_kernel(sizes, *refs):
    X, Y, Z = sizes
    cx = X // 4
    yfine, left_ref, right_ref, yd_ref, yu_ref, xl_ref, xr_ref, mask, force_ref = refs[:9]
    velo_out, press_out = refs[9:11]
    force, step, state, mid, sems = refs[11:]
    ex, ey, fy = 4, 16, 8
    deep = cx + 10

    copies = []

    def copy(src, dst):
        made = pltpu.make_async_copy(src, dst, sems.at[len(copies)])
        made.start()
        copies.append(made)
        return made

    second = []
    for field in range(3):
        second.append(copy(force_ref.at[field], force.at[field, pl.ds(ex, X), pl.ds(fy, Y), :]))
    for ref, high in ((xl_ref, False), (xr_ref, True)):
        number = 0
        for field, depth in x_depths:
            x = ex + X if high else ex - depth
            target = step.at[pl.ds(x, depth), pl.ds(fy, Y), :] if field == 3 else force.at[field, pl.ds(x, depth), pl.ds(fy, Y), :]
            second.append(copy(ref.at[pl.ds(number, depth)], target))
            number += depth

    wide = Y + 16
    wide_rows = pl.ds(ey - 8, wide)

    def stretch_x(m, carry):
        for field in range(4):
            low, here, high = yfine[field, m], yfine[field, m + 1], yfine[field, m + 2]
            state[field, 4 * m, wide_rows, :] = 0.375 * low + 0.625 * here
            state[field, 4 * m + 1, wide_rows, :] = 0.125 * low + 0.875 * here
            state[field, 4 * m + 2, wide_rows, :] = 0.875 * here + 0.125 * high
            state[field, 4 * m + 3, wide_rows, :] = 0.625 * here + 0.375 * high
        return carry

    lax.fori_loop(0, cx + 2, stretch_x, 0)

    for made in second:
        made.wait()
    for x in range(X):
        step[ex + x, pl.ds(fy, Y), :] = step_of(mask[x])
    for ref, high in ((yd_ref, False), (yu_ref, True)):
        number = 0
        for field, depth in y_depths:
            for row in range(depth):
                y = fy + Y + row if high else fy - depth + row
                for x in range(X):
                    place = number * X + x
                    line = ref[-(-5 * cx // 8) + 2 + place // 8, pl.ds(place % 8, 1), :]
                    if field == 3:
                        step[ex + x, pl.ds(y, 1), :] = line
                    else:
                        force[field, ex + x, pl.ds(y, 1), :] = line
                number += 1
        for side, corner_ref in enumerate((left_ref, right_ref)):
            for row, (field, dx, dy) in enumerate(corner_cells):
                x = ex - dx if side == 0 else ex + X - 1 + dx
                y = fy + Y - 1 + dy if high else fy - dy
                line = corner_ref[16 if high else 15, pl.ds(row, 1), :]
                if field == 3:
                    step[x, pl.ds(y, 1), :] = line
                else:
                    force[field, x, pl.ds(y, 1), :] = line

    pair_sum, pair_gap = neighbour_matrices(Z, 1)

    def move(old, new, x, count, components, start, size):
        rows, above, below = pl.ds(ey + start, size), pl.ds(ey + start + 1, size), pl.ds(ey + start - 1, size)
        source_rows = pl.ds(fy + start, size)
        planes, right, left = pl.ds(x, count), pl.ds(x + 1, count), pl.ds(x - 1, count)
        shape = (count, size, Z)
        ratio = step[planes, source_rows, :]
        middles = [old[a, planes, rows, :] for a in components]
        sums = apply(pair_sum, jnp.concatenate([flat(v) for v in middles], 0))
        for number, a in enumerate(components):
            if a == 0:
                slope = state[3, right, rows, :] - state[3, left, rows, :]
            elif a == 1:
                slope = state[3, planes, above, :] - state[3, planes, below, :]
            elif 0:
                slope = apply(pair_gap, flat(state[3, planes, rows, :])).reshape(shape)
            else:
                press = state[3, planes, rows, :]
                slope = roll(press, -1) - roll(press, 1)
            near = old[a, right, rows, :] + old[a, left, rows, :]
            near = near + (old[a, planes, above, :] + old[a, planes, below, :])
            near = near + sums[number * count * size : (number + 1) * count * size].reshape(shape)
            source = force[a, planes, source_rows, :]
            if a == 0:
                source = source + mean_drive
            source = source - 0.5 * slope + near
            new[a, planes, rows, :] = keep * middles[number] + ratio * source

    def divergence(vel, x, count, start, size):
        rows, above, below = pl.ds(ey + start, size), pl.ds(ey + start + 1, size), pl.ds(ey + start - 1, size)
        planes, right, left = pl.ds(x, count), pl.ds(x + 1, count), pl.ds(x - 1, count)
        total = (vel[0, right, rows, :] - vel[0, left, rows, :]) + (vel[1, planes, above, :] - vel[1, planes, below, :])
        along_z = vel[2, planes, rows, :]
        if 1:
            total = total + apply(pair_gap, flat(along_z)).reshape(total.shape)
        else:
            total = total + (roll(along_z, -1) - roll(along_z, 1))
        return total * (0.5 * pressure_step)

    def loop(low, high, most, body):
        count = max(n for n in range(1, most + 1) if (high - low) % n == 0)

        def run(number, carry):
            body(low + number * count, count)
            return carry

        lax.fori_loop(0, (high - low) // count, run, 0)

    loop(1, X + 7, 30, lambda x, count: move(state, mid, x, count, (0, 1, 2), -8, wide))

    def press_first(x, count):
        planes = pl.ds(x, count)
        state[3, planes, wide_rows, :] = state[3, planes, wide_rows, :] - divergence(mid, x, count, -8, wide)

    loop(2, X + 6, 28, press_first)
    move(mid, state, ex - 1, 1, (0,), 0, Y)
    move(mid, state, ex + X, 1, (0,), 0, Y)

    def second_move(x, count):
        move(mid, state, x, count, (0, 2), 0, Y)
        move(mid, state, x, count, (1,), -8, wide)

    loop(ex, ex + X, 24, second_move)
    inner = pl.ds(ey, Y)
    last = [copy(state.at[a, pl.ds(ex, X), inner, :], velo_out.at[a]) for a in range(3)]

    def press_second(x, count):
        planes = pl.ds(x, count)
        step[planes, pl.ds(fy, Y), :] = state[3, planes, inner, :] - divergence(state, x, count, 0, Y)

    loop(ex, ex + X, 24, press_second)
    last.append(copy(step.at[pl.ds(ex, X), pl.ds(fy, Y), :], press_out))
    for made in last:
        made.wait()


def relay_kernel(sizes, mu_ref, own_ref, md_ref, right_ref, left_ref):
    cx, cy, Z = sizes[0] // 4, sizes[1] // 4, sizes[2]
    own_tiles = -(-5 * cx // 8)
    for ref, start, corner in ((right_ref, cx - 5, own_tiles), (left_ref, 0, own_tiles + 1)):
        blank = jnp.zeros((5, cy - 5, Z), jnp.float32)
        ref[pl.ds(0, 5), pl.ds(0, cy - 5), :] = blank
        ref[pl.ds(10, 5), pl.ds(5, cy - 5), :] = blank
        for plane in range(5):
            rows = pl.ds(5 * (start + plane), 5)
            ref[plane, pl.ds(cy - 5, 5), :] = md_ref.reshape(-1, Z)[rows, :]
            ref[10 + plane, pl.ds(0, 5), :] = mu_ref.reshape(-1, Z)[rows, :]
        ref[pl.ds(5, 5)] = own_ref[pl.ds(start, 5)]
        ref[15] = md_ref[corner]
        ref[16] = mu_ref[corner]


def shift(value, axis, by):
    count = lax.axis_size(axis)
    return lax.ppermute(value, axis, [(i, (i + by) % count) for i in range(count)])


def shards(solid_mask, forcing):
    X, Y, Z = sizes = solid_mask.shape
    cx, cy = X // 4, Y // 4
    f32 = jnp.float32
    made = jax.ShapeDtypeStruct
    vmem = pltpu.VMEM
    anywhere = pl.BlockSpec(memory_space=pl.ANY)
    near = pl.BlockSpec(memory_space=vmem)
    message = made((-(-5 * cx // 8) + 2 + 10 * X // 8, 8, Z), f32)
    planes = made((10, Y, Z), f32)
    own, mp, mm, xp, xm, mask, force = pl.pallas_call(
        functools.partial(pack_kernel, sizes),
        out_shape=(made((cx, 8, Z), f32), message, message, planes, planes, made((X * Y, Z), jnp.int32), made((3 * X * Y, Z), f32)),
        in_specs=[pl.BlockSpec(memory_space=pltpu.HBM)] * 2,
        out_specs=[near] * 7,
        scratch_shapes=[vmem((4, cx, Y, Z), f32), pltpu.SemaphoreType.DMA((4,))],
        compiler_params=pltpu.CompilerParams(vmem_limit_bytes=12 * 2**20),
        name="pack",
    )(
        pltpu.with_memory_space_constraint(solid_mask.reshape(X * Y, Z), pltpu.HBM),
        pltpu.with_memory_space_constraint(forcing.reshape(3 * X * Y, Z), pltpu.HBM),
    )
    md = shift(mp, "dev", 1)
    mu = shift(mm, "dev", -1)
    xl = shift(xp, "grp", 1)
    xr = shift(xm, "grp", -1)
    joined = made((17, 8, Z), f32)
    to_right, to_left = pl.pallas_call(
        functools.partial(relay_kernel, sizes),
        out_shape=(joined, joined),
        in_specs=[near] * 3,
        out_specs=[near] * 2,
        compiler_params=pltpu.CompilerParams(vmem_limit_bytes=2 * 2**20),
        name="relay",
    )(mu, own, md)
    left = shift(to_right, "grp", 1)
    right = shift(to_left, "grp", -1)
    tall, deep = 3 * cy, cx + 10
    yfine = pl.pallas_call(
        functools.partial(coarse_kernel, sizes),
        out_shape=made((4, cx + 4, Y + 16, Z), f32),
        in_specs=[near] * 6,
        out_specs=near,
        scratch_shapes=[
            vmem((deep, tall, Z), f32),
            vmem((3, deep, tall, Z), f32),
            vmem((deep, tall, Z), f32),
            vmem((2, 3, deep, tall + 2 * cy, Z), f32),
            vmem((deep, tall + 2 * cy, Z), f32),
            vmem((4, cx + 4, tall, Z), f32),
        ],
        compiler_params=pltpu.CompilerParams(vmem_limit_bytes=16 * 2**20),
        name="coarse",
    )(left, right, md, own, mm, mu)
    return pl.pallas_call(
        functools.partial(solve_kernel, sizes),
        out_shape=(made((3, X, Y, Z), f32), made((X, Y, Z), f32)),
        in_specs=[near] * 9,
        out_specs=(anywhere, anywhere),
        scratch_shapes=[
            vmem((3, X + 8, Y + 16, Z), f32),
            vmem((X + 8, Y + 16, Z), f32),
            vmem((4, X + 8, Y + 32, Z), f32),
            vmem((3, X + 8, Y + 32, Z), f32),
            pltpu.SemaphoreType.DMA((20,)),
        ],
        compiler_params=pltpu.CompilerParams(vmem_limit_bytes=32 * 2**20),
        name="solve",
    )(yfine, left, right, md, mu, xl, xr, mask.reshape(X, Y, Z), force.reshape(3, X, Y, Z))


def solution(mesh):
    in_specs = (P("grp", "dev", None), P(None, "grp", "dev", None))
    out_specs = (P(None, "grp", "dev", None), P("grp", "dev", None))
    return jax.shard_map(shards, mesh=mesh, in_specs=in_specs, out_specs=out_specs, check_vma=False)
```
